32 devices in a mesh: gx: 4 (over y, x), gy: 8 (over z, core).
Axes of the slice: x: 2, y: 2, z: 4, core: 2. Of those that a mesh axis runs over, the one named last changes fastest.
Arguments:
- noise: float32 [8, 16, 4, 128], P('gx', 'gy'), may hold values from -4 to 4
- w_first: bfloat16 [16, 1, 3, 3, 3, 3], replicated, may hold values from -0.625 to 0.625
- b_first: float32 [16], replicated, may hold values from -2 to 2
- w_middle: bfloat16 [16, 16, 3, 3, 3, 3], replicated, may hold values from -0.15625 to 0.15625
- b_middle: float32 [16], replicated, may hold values from -2 to 2
- w_last: bfloat16 [2, 16, 3, 3, 3, 3], replicated, may hold values from -0.15625 to 0.15625
- b_last: float32 [2], replicated, may hold values from -2 to 2
Outputs:
- field: float32 [8, 16, 4, 128], P('gx', 'gy')
- noise_grad: float32 [8, 16, 4, 128], P('gx', 'gy')
- loss: float32 [], replicated
- w_first_grad: float32 [16, 1, 3, 3, 3, 3], replicated
- b_first_grad: float32 [16], replicated
- w_middle_grad: float32 [16, 16, 3, 3, 3, 3], replicated
- b_middle_grad: float32 [16], replicated
- w_last_grad: float32 [2, 16, 3, 3, 3, 3], replicated
- b_last_grad: float32 [2], replicated
The draws below stay inside these ranges and needn't reach their ends.
All inputs are finite; a program needn't handle non-finite values.
Results may differ from the reference program's by a relative error of at most 0.0074.
Values may be sent and summed in bfloat16 or wider, within the bound.
A program may use at most 128 MiB of HBM per device.

```python
import jax
import jax.numpy as jnp
from jax import lax

CH = 16
LT = 4
LZ = 128
LX = 8
LY = 16


def block_scale(stream_key, dims, split, smallest, largest):
    factor_of = 1.0
    for position, parts in split:
        steps = jax.random.uniform(jax.random.fold_in(jax.random.fold_in(stream_key, 6), position), (parts,), jnp.float32, smallest / len(split), largest / len(split))
        factor_of = factor_of * jnp.repeat(jnp.exp(steps), dims[position] // parts).reshape((-1,) + (1,) * (len(dims) - 1 - position))
    return factor_of


def gaussian(stream_key, shape, scale, bound, shards=(), kind=jnp.bfloat16):
    entries = scale * jax.random.normal(stream_key, shape, jnp.float32)
    if shards:
        entries = entries * block_scale(stream_key, shape, shards, -0.22, 0.18)
    return jnp.clip(entries, -bound, bound).astype(kind)


def setup_inputs(seed: int = 0) -> dict:
    splits = jax.random.split(jax.random.key(seed), 8)
    return {
        "noise": gaussian(splits[0], (LX, LY, LT, LZ), 1.0, 4.0, ((0, 4), (1, 8)), jnp.float32),
        "w_first": gaussian(splits[1], (CH, 1, 3, 3, 3, 3), 81 ** -0.5, 0.625),
        "b_first": gaussian(splits[2], (CH,), 0.5, 2.0, (), jnp.float32),
        "w_middle": gaussian(splits[3], (CH, CH, 3, 3, 3, 3), (CH * 81) ** -0.5, 0.15625),
        "b_middle": gaussian(splits[4], (CH,), 0.5, 2.0, (), jnp.float32),
        "w_last": gaussian(splits[5], (2, CH, 3, 3, 3, 3), (CH * 81) ** -0.5, 0.15625),
        "b_last": gaussian(splits[6], (2,), 0.5, 2.0, (), jnp.float32),
    }


HOPPING = 0.15
QUARTIC = 0.1

def parity_mask(shape, offset_x, offset_y):
    index_x = jnp.arange(shape[0], dtype=jnp.int32) + offset_x
    index_y = jnp.arange(shape[1], dtype=jnp.int32) + offset_y
    index_t = jnp.arange(shape[2], dtype=jnp.int32)
    index_z = jnp.arange(shape[3], dtype=jnp.int32)
    summed = index_x[:, None, None, None] + index_y[None, :, None, None] + index_t[None, None, :, None] + index_z[None, None, None, :]
    return jnp.where(summed % 2 == 0, 1.0, 0.0).astype(jnp.float32)

def conv_block(padded, kernel):
    width_x = padded.shape[0] - 2
    width_y = padded.shape[1] - 2
    summed = None
    for a in range(3):
        for b in range(3):
            window = padded[a:a + width_x, b:b + width_y]
            flattened = window.reshape((width_x * width_y,) + window.shape[2:])
            partial_out = lax.conv_general_dilated(flattened, kernel[:, :, a, b], (1, 1), 'VALID', preferred_element_type=jnp.float32)
            summed = partial_out if summed is None else summed + partial_out
    return summed.reshape((width_x, width_y) + summed.shape[1:])

def kernel_grad(padded, cotangent):
    width_x = cotangent.shape[0]
    width_y = cotangent.shape[1]
    flat_cot = cotangent.reshape((width_x * width_y,) + cotangent.shape[2:])
    pieces = []
    for a in range(3):
        for b in range(3):
            window = padded[a:a + width_x, b:b + width_y]
            flattened = window.reshape((width_x * width_y,) + window.shape[2:])
            pieces.append(lax.conv_general_dilated(flattened, flat_cot, (1, 1), 'VALID', dimension_numbers=('CNHW', 'IOHW', 'NCHW'), preferred_element_type=jnp.float32))
    stacked = jnp.stack(pieces).reshape((3, 3) + pieces[0].shape)
    return jnp.transpose(stacked, (3, 2, 0, 1, 4, 5))

def flip_kernel(kernel):
    return jnp.transpose(kernel[:, :, ::-1, ::-1, ::-1, ::-1], (1, 0, 2, 3, 4, 5))

def wrap_all(field):
    return jnp.pad(field, ((1, 1), (1, 1), (0, 0), (1, 1), (1, 1)), mode='wrap')

def channel_bias(bias):
    return bias[None, None, :, None, None]

def reference(noise, w_first, b_first, w_middle, b_middle, w_last, b_last):
    frozen = parity_mask(noise.shape, 0, 0)
    active = 1.0 - frozen
    sites = float(noise.size)
    inputs = (frozen * noise).astype(jnp.bfloat16)[:, :, None]
    hidden_one = jnp.tanh(conv_block(wrap_all(inputs), w_first) + channel_bias(b_first)).astype(jnp.bfloat16)
    hidden_two = jnp.tanh(conv_block(wrap_all(hidden_one), w_middle) + channel_bias(b_middle)).astype(jnp.bfloat16)
    head_out = conv_block(wrap_all(hidden_two), w_last) + channel_bias(b_last)
    log_scale = jnp.tanh(head_out[:, :, 0])
    offset_field = head_out[:, :, 1]
    growth = jnp.exp(log_scale)
    field = frozen * noise + active * (noise * growth + offset_field)
    upward = jnp.roll(field, -1, 0) + jnp.roll(field, -1, 1) + jnp.roll(field, -1, 2) + jnp.roll(field, -1, 3)
    downward = jnp.roll(field, 1, 0) + jnp.roll(field, 1, 1) + jnp.roll(field, 1, 2) + jnp.roll(field, 1, 3)
    squared = field * field
    density = -2.0 * HOPPING * field * upward + squared + QUARTIC * (squared - 1.0) * (squared - 1.0)
    summed = jnp.sum(-0.5 * noise * noise - active * log_scale + density)
    force_field = -2.0 * HOPPING * (upward + downward) + 2.0 * field + 4.0 * QUARTIC * field * (squared - 1.0)
    d_scale = active * (force_field * noise * growth - 1.0) * (1.0 - log_scale * log_scale)
    d_offset = active * force_field
    cot_last = jnp.stack([d_scale, d_offset], axis=2).astype(jnp.bfloat16)
    grad_last = kernel_grad(wrap_all(hidden_two), cot_last)
    bias_last = lax.optimization_barrier(jnp.sum(cot_last.astype(jnp.float32), axis=(0, 1, 3, 4)))
    two_float = hidden_two.astype(jnp.float32)
    cot_middle = (conv_block(wrap_all(cot_last), flip_kernel(w_last)) * (1.0 - two_float * two_float)).astype(jnp.bfloat16)
    grad_middle = kernel_grad(wrap_all(hidden_one), cot_middle)
    bias_middle = lax.optimization_barrier(jnp.sum(cot_middle.astype(jnp.float32), axis=(0, 1, 3, 4)))
    one_float = hidden_one.astype(jnp.float32)
    cot_first = (conv_block(wrap_all(cot_middle), flip_kernel(w_middle)) * (1.0 - one_float * one_float)).astype(jnp.bfloat16)
    grad_first = kernel_grad(wrap_all(inputs), cot_first)
    bias_first = lax.optimization_barrier(jnp.sum(cot_first.astype(jnp.float32), axis=(0, 1, 3, 4)))
    d_inputs = conv_block(wrap_all(cot_first), flip_kernel(w_first))
    noise_grad = frozen * d_inputs[:, :, 0] + force_field * (frozen + active * growth) - noise
    return (field, noise_grad, summed / sites, grad_first / sites, bias_first / sites, grad_middle / sites, bias_middle / sites, grad_last / sites, bias_last / sites)
```

```python
import functools

import jax
import jax.numpy as jnp
from jax import lax
from jax.experimental import pallas as pl
from jax.experimental.pallas import tpu as pltpu
from jax.sharding import PartitionSpec as P

HOPPING = 0.15
QUARTIC = 0.1
MESH = pl.DeviceIdType.MESH
F32 = jnp.float32
BF16 = jnp.bfloat16
OFFSETS = [(dx, dy) for dx in range(-2, 3) for dy in range(-2, 3) if (dx, dy) != (0, 0)]
PAIRS = [(y, t) for y in range(2) for t in range(4)]


def dot(a, b):
    return jnp.dot(a, b, preferred_element_type=F32)


def dot_nt(a, b):
    return lax.dot_general(a, b, (((1,), (1,)), ((), ())), preferred_element_type=F32)


def roll_z(v, step):
    if step == 0:
        return v
    parts = [
        pltpu.roll(v[:, k : k + 128], (-step) % 128, 1) for k in range(0, v.shape[1], 128)
    ]
    return parts[0] if len(parts) == 1 else jnp.concatenate(parts, axis=1)


def iota(shape, dim):
    return lax.broadcasted_iota(jnp.int32, shape, dim)


def select_matrix(rows, target):
    lanes = target.shape[1]
    return jnp.where(iota((rows, lanes), 0) == target, 1.0, 0.0).astype(BF16)


def taps_channels(y, t):
    lane = iota((1, 256), 1)
    b = (lane >> 6) - y
    c = (((lane >> 4) & 3) - t + 1) & 3
    ok = (b >= 0) & (b <= 2) & (c <= 2)
    return select_matrix(144, jnp.where(ok, b * 48 + c * 16 + (lane & 15), -1))


def taps_single(y, t):
    lane = iota((1, 144), 1)
    b = ((lane >> 2) & 3) - y
    c = ((lane & 3) - t + 1) & 3
    ok = (b >= 0) & (b <= 2) & (c <= 2)
    return select_matrix(81, jnp.where(ok, (lane >> 4) * 9 + b * 3 + c, -1))


def taps_heads(y, t):
    lane = iota((1, 432), 1)
    group = sum((lane >= 48 * k).astype(jnp.int32) for k in range(1, 9))
    rest = lane - 48 * group
    b = 2 * (rest >> 4) + ((rest >> 2) & 1) - y - 1
    c = ((rest & 3) - t + 1) & 3
    ok = (b >= 0) & (b <= 2) & (c <= 2)
    target = group * 18 + ((rest >> 3) & 1) * 9 + b * 3 + c
    return select_matrix(162, jnp.where(ok, target, -1))


def split(v):
    high = v.astype(BF16)
    return high, (v - high.astype(F32)).astype(BF16)


def kernel(
    nx, ny, noise_ref, wall_ref, w1_ref, w3t_ref, b1_ref, b2_ref, b3_ref,
    field_ref, ngrad_ref, pack_ref,
    win, inr, clw, clr, g2, g2t, g1, g3t, h1, h2, cm, cf, fld,
    send_a, recv_a, send_b, recv_b,
):
    ix, iy = lax.axis_index("gx"), lax.axis_index("gy")

    def peer(dx, dy):
        return (lax.rem(ix + dx + 2 * nx, nx), lax.rem(iy + dy + 2 * ny, ny))

    def exchange(ref, rows, send, recv):
        copies = []
        for k, (dx, dy) in enumerate(OFFSETS):
            copies.append(
                pltpu.make_async_remote_copy(
                    src_ref=ref.at[pl.ds(2 * rows, rows), pl.ds(512, 256)],
                    dst_ref=ref.at[pl.ds((2 - dy) * rows, rows), pl.ds((2 - dx) * 256, 256)],
                    send_sem=send.at[k],
                    recv_sem=recv.at[k],
                    device_id=peer(dx, dy),
                    device_id_type=MESH,
                )
            )
        return copies

    for x in range(2):
        for y in range(2):
            win[pl.ds(16 + 4 * y, 4), pl.ds(512 + 128 * x, 128)] = noise_ref[x, y]

    barrier = pltpu.get_barrier_semaphore()
    for dx, dy in OFFSETS:
        pl.semaphore_signal(barrier, inc=1, device_id=peer(dx, dy), device_id_type=MESH)
    pl.semaphore_wait(barrier, len(OFFSETS))
    first = exchange(win, 8, send_a, recv_a)
    for copy in first:
        copy.start()

    wall = wall_ref[...]
    w1 = w1_ref[...]
    w3t = w3t_ref[...]
    small = []
    for n, (y, t) in enumerate(PAIRS):
        full = dot(wall, taps_channels(y, t)).astype(BF16)
        for a in range(3):
            for d in range(3):
                g2[a, pl.ds(d * 128 + n * 16, 16), :] = full[(3 * a + d) * 16 : (3 * a + d) * 16 + 16]
                g2t[a, pl.ds(d * 128 + n * 16, 16), :] = full[
                    144 + (3 * a + d) * 16 : 144 + (3 * a + d) * 16 + 16
                ]
        small.append(full[288:320])
        g1[pl.ds(n * 16, 16), :] = dot(w1, taps_single(y, t)).astype(BF16)
        g3t[pl.ds(n * 16, 16), :] = dot(w3t, taps_heads(y, t)).astype(BF16)
    small = jnp.concatenate(small, axis=0)
    row = iota((216, 256), 0)
    order = jnp.where((row & 7) * 32 + (row >> 3) == iota((216, 256), 1), 1.0, 0.0).astype(BF16)
    small = dot(order, small).astype(BF16)
    g3 = [small[48 * a : 48 * a + 48] for a in range(3)]
    g1t = [small[144 + 24 * a : 168 + 24 * a] for a in range(3)]
    b1, b2 = b1_ref[...], b2_ref[...]
    bias1 = jnp.concatenate([b1] * 8, axis=0)
    bias2 = jnp.concatenate([b2] * 8, axis=0)

    for copy in first:
        copy.wait()

    noise_all = win[...]
    parity = (iota((40, 1280), 0) >> 2) + iota((40, 1280), 0) + (iota((40, 1280), 1) >> 7) + iota((40, 1280), 1)
    inputs = jnp.where((parity & 1) == 0, noise_all, 0.0).astype(BF16).astype(F32)
    for d in range(3):
        inr[d] = roll_z(inputs, d - 1)
    for j in range(4):
        stack = jnp.concatenate(
            [
                inr[d, pl.ds(8 * j, 16), pl.ds(128 * a, 1024)]
                for d in range(3)
                for a in range(3)
            ],
            axis=0,
        ).astype(BF16)
        h1[pl.ds(128 * j, 128), :] = jnp.tanh(dot(g1[...], stack) + bias1).astype(BF16)

    def conv(mats, ref, start, width, rows):
        out = None
        for a in range(3):
            part = dot(mats[a], ref[pl.ds(start, 256), pl.ds(128 * a, width)])
            out = part if out is None else out + part
        total = out[rows : 2 * rows]
        for d in (0, 2):
            total = total + roll_z(out[d * rows : (d + 1) * rows], d - 1)
        return total

    for k in range(3):
        h2[pl.ds(128 * k, 128), :] = jnp.tanh(
            conv(g2, h1, 128 * k, 768, 128) + bias2
        ).astype(BF16)

    scales, growths = [], []
    for k in range(2):
        head = conv(g3, h2, 128 * k, 512, 16)
        log_scale = jnp.tanh(head[:8] + b3_ref[0])
        offset = head[8:] + b3_ref[1]
        noise = win[pl.ds(12 + 8 * k, 8), pl.ds(384, 512)]
        growth = jnp.exp(log_scale)
        r, l = iota((8, 512), 0), iota((8, 512), 1)
        even = (((r >> 2) + r + (l >> 7) + l) & 1) == 0
        fld[pl.ds(8 * k, 8), :] = jnp.where(even, noise, noise * growth + offset)
        scales.append(log_scale)
    log_scale = jnp.concatenate([scales[0][4:], scales[1][:4]], axis=0)[:, 128:384]
    growth = jnp.exp(log_scale)
    noise = win[pl.ds(16, 8), pl.ds(512, 256)]
    field = fld[pl.ds(4, 8), pl.ds(128, 256)]
    r, l = iota((8, 256), 0), iota((8, 256), 1)
    frozen = (((r >> 2) + r + (l >> 7) + l) & 1) == 0
    active = jnp.where(frozen, 0.0, 1.0)
    t_up = jnp.concatenate([field[1:4], field[0:1], field[5:8], field[4:5]], axis=0)
    t_down = jnp.concatenate([field[3:4], field[0:3], field[7:8], field[4:7]], axis=0)
    upward = (
        fld[pl.ds(4, 8), pl.ds(256, 256)] + fld[pl.ds(8, 8), pl.ds(128, 256)]
        + t_up + roll_z(field, 1)
    )
    downward = (
        fld[pl.ds(4, 8), pl.ds(0, 256)] + fld[pl.ds(0, 8), pl.ds(128, 256)]
        + t_down + roll_z(field, -1)
    )
    squared = field * field
    density = (
        -2.0 * HOPPING * field * upward + squared + QUARTIC * (squared - 1.0) * (squared - 1.0)
    )
    loss = jnp.sum(
        jnp.sum(-0.5 * noise * noise - active * log_scale + density, axis=1, keepdims=True),
        axis=0, keepdims=True,
    )
    force = (
        -2.0 * HOPPING * (upward + downward) + 2.0 * field + 4.0 * QUARTIC * field * (squared - 1.0)
    )
    d_scale = active * (force * noise * growth - 1.0) * (1.0 - log_scale * log_scale)
    d_offset = active * force
    cot_last = jnp.concatenate([d_scale, d_offset], axis=0).astype(BF16)
    clw[pl.ds(32, 16), pl.ds(512, 256)] = cot_last
    second = exchange(clw, 16, send_b, recv_b)
    for copy in second:
        copy.start()
    for x in range(2):
        for y in range(2):
            field_ref[x, y] = field[4 * y : 4 * y + 4, 128 * x : 128 * x + 128]

    cot_f = cot_last.astype(F32)
    bias_last = jnp.sum(cot_f, axis=1, keepdims=True)
    bias_last = jnp.concatenate(
        [jnp.sum(bias_last[:8], axis=0, keepdims=True), jnp.sum(bias_last[8:], axis=0, keepdims=True)],
        axis=0,
    )
    turned = jnp.concatenate([roll_z(cot_f, 1 - d) for d in range(3)], axis=0).astype(BF16)
    row, col = iota((64, 48), 0), iota((64, 48), 1)
    order = jnp.where((row & 7) * 8 + (row >> 3) == col, 1.0, 0.0).astype(BF16)
    turned = dot(order, turned).astype(BF16)
    last_products = [
        dot_nt(turned, h2[pl.ds(64, 256), pl.ds(128 * (a + 1), 256)]) for a in range(3)
    ]

    for copy in second:
        copy.wait()

    everywhere = clw[...].astype(F32)
    for d in range(3):
        clr[d] = roll_z(everywhere, d - 1).astype(BF16)
    for k in range(3):
        stack = jnp.concatenate(
            [
                clr[d, pl.ds(16 * k, 48), pl.ds(128 * (a + 1), 768)]
                for d in range(3)
                for a in range(3)
            ],
            axis=0,
        )
        hidden = h2[pl.ds(128 * k, 128), :].astype(F32)
        cm[pl.ds(128 * k, 128), :] = (dot(g3t[...], stack) * (1.0 - hidden * hidden)).astype(BF16)

    mine = cm[pl.ds(128, 128), pl.ds(256, 256)].astype(F32)
    bias_mid = jnp.sum(mine, axis=1, keepdims=True)
    bias_mid = sum(bias_mid[16 * n : 16 * n + 16] for n in range(8))
    turned = jnp.concatenate([roll_z(mine, 1 - d) for d in range(3)], axis=0).astype(BF16)
    products = [dot_nt(turned, h1[pl.ds(128, 256), pl.ds(128 * (a + 2), 256)]) for a in range(3)]
    folded = None
    for n, (y, t) in enumerate(PAIRS):
        piece = jnp.concatenate(
            [
                products[a][d * 128 + n * 16 : d * 128 + n * 16 + 16]
                for a in range(3)
                for d in range(3)
            ]
            + [last_products[a][8 * n : 8 * n + 8] for a in range(3)],
            axis=0,
        )
        high, low = split(piece)
        matrix = taps_channels(y, t)
        part = dot_nt(high, matrix) + dot_nt(low, matrix)
        folded = part if folded is None else folded + part
    pack_ref[pl.ds(0, 168), :] = folded

    for k in range(2):
        hidden = h1[pl.ds(128 * (k + 1), 128), pl.ds(256, 512)].astype(F32)
        cf[pl.ds(128 * k, 128), :] = (
            conv(g2t, cm, 128 * k, 512, 128) * (1.0 - hidden * hidden)
        ).astype(BF16)
    mine = cf[pl.ds(64, 128), pl.ds(128, 256)]
    bias_first = jnp.sum(mine.astype(F32), axis=1, keepdims=True)
    bias_first = sum(bias_first[16 * n : 16 * n + 16] for n in range(8))
    stack = jnp.concatenate(
        [inr[d, pl.ds(12, 16), pl.ds(128 * (a + 3), 256)] for d in range(3) for a in range(3)], axis=0
    ).astype(BF16)
    product = dot_nt(mine, stack)
    folded = None
    for n, (y, t) in enumerate(PAIRS):
        high, low = split(product[16 * n : 16 * n + 16])
        matrix = taps_single(y, t)
        part = dot_nt(high, matrix) + dot_nt(low, matrix)
        folded = part if folded is None else folded + part
    pad = jnp.zeros((14, 1), F32)
    pack_ref[pl.ds(168, 16), :] = jnp.concatenate(
        [
            folded, bias_mid, bias_first, jnp.concatenate([bias_last, pad], axis=0),
            jnp.concatenate([loss, pad, jnp.zeros((1, 1), F32)], axis=0), jnp.zeros((16, 59), F32),
        ],
        axis=1,
    )

    back = conv(g1t, cf, 0, 256, 8)
    result = jnp.where(frozen, back, 0.0) + force * jnp.where(frozen, 1.0, growth) - noise
    for x in range(2):
        for y in range(2):
            ngrad_ref[x, y] = result[4 * y : 4 * y + 4, 128 * x : 128 * x + 128]


def local(nx, ny, noise, w_first, b_first, w_middle, b_middle, w_last, b_last):
    sites = float(noise.size * nx * ny)
    wm = jnp.transpose(w_middle, (2, 5, 0, 3, 4, 1)).reshape(144, 144)
    wmt = jnp.transpose(w_middle[:, :, ::-1, ::-1, ::-1, ::-1], (2, 5, 1, 3, 4, 0)).reshape(144, 144)
    wl = jnp.transpose(w_last, (2, 5, 0, 3, 4, 1)).reshape(18, 144)
    wft = jnp.transpose(w_first[:, 0, ::-1, ::-1, ::-1, ::-1], (1, 4, 2, 3, 0)).reshape(9, 144)
    wall = jnp.concatenate([wm, wmt, wl, wft, jnp.zeros((5, 144), BF16)], axis=0)
    w1 = jnp.transpose(w_first[:, 0], (0, 4, 1, 2, 3)).reshape(16, 81)
    w3t = jnp.transpose(w_last[:, :, ::-1, ::-1, ::-1, ::-1], (1, 5, 2, 0, 3, 4)).reshape(16, 162)
    vmem = pl.BlockSpec(memory_space=pltpu.VMEM)
    smem = pl.BlockSpec(memory_space=pltpu.SMEM)
    field, ngrad, pack = pl.pallas_call(
        functools.partial(kernel, nx, ny),
        out_shape=(
            jax.ShapeDtypeStruct(noise.shape, F32),
            jax.ShapeDtypeStruct(noise.shape, F32),
            jax.ShapeDtypeStruct((184, 144), F32),
        ),
        in_specs=[vmem] * 6 + [smem],
        out_specs=(vmem, vmem, vmem),
        scratch_shapes=[
            pltpu.VMEM((40, 1280), F32),
            pltpu.VMEM((3, 40, 1280), F32),
            pltpu.VMEM((80, 1280), BF16),
            pltpu.VMEM((3, 80, 1280), BF16),
            pltpu.VMEM((3, 384, 256), BF16),
            pltpu.VMEM((3, 384, 256), BF16),
            pltpu.VMEM((128, 144), BF16),
            pltpu.VMEM((128, 432), BF16),
            pltpu.VMEM((512, 1024), BF16),
            pltpu.VMEM((384, 768), BF16),
            pltpu.VMEM((384, 768), BF16),
            pltpu.VMEM((256, 512), BF16),
            pltpu.VMEM((16, 512), F32),
        ]
        + [pltpu.SemaphoreType.DMA((24,))] * 4,
        compiler_params=pltpu.CompilerParams(
            collective_id=0, has_side_effects=True, vmem_limit_bytes=32 * 1024 * 1024
        ),
    )(noise, wall, w1, w3t, b_first[:, None], b_middle[:, None], b_last)
    pack = lax.psum(pack, ("gx", "gy")) / sites
    middle = jnp.transpose(pack[:144].reshape(3, 3, 16, 3, 3, 16), (2, 5, 0, 3, 4, 1))
    last = jnp.transpose(
        pack[144:168].reshape(3, 8, 3, 3, 16)[:, :6].reshape(3, 3, 2, 3, 3, 16), (2, 5, 0, 3, 4, 1)
    )
    extra = pack[168:184]
    first = jnp.transpose(extra[:, :81].reshape(16, 3, 3, 3, 3), (0, 2, 3, 4, 1))[:, None]
    return (
        field, ngrad, extra[0, 84], first, extra[:, 82], middle, extra[:, 81], last, extra[:2, 83],
    )


def solution(mesh):
    placed = (P("gx", "gy", None, None), P(), P(), P(), P(), P(), P())
    return jax.shard_map(
        functools.partial(local, mesh.shape["gx"], mesh.shape["gy"]),
        mesh=mesh,
        in_specs=placed,
        out_specs=(
            P("gx", "gy", None, None), P("gx", "gy", None, None), P(), P(), P(), P(), P(), P(), P(),
        ),
        check_vma=False,
    )
```

```python
import functools

import jax
import jax.numpy as jnp
from jax import lax
from jax.experimental import pallas as pl
from jax.experimental.pallas import tpu as pltpu
from jax.sharding import PartitionSpec as P

HOPPING = 0.15
QUARTIC = 0.1
MESH = pl.DeviceIdType.MESH
F32 = jnp.float32
BF16 = jnp.bfloat16
OFFSETS = [(dx, dy) for dx in range(-2, 3) for dy in range(-2, 3) if (dx, dy) != (0, 0)]
CHUNKS = 26
PAIRS = [(y, t) for y in range(2) for t in range(4)]


def dot(a, b):
    return jnp.dot(a, b, preferred_element_type=F32)


def dot_nt(a, b):
    return lax.dot_general(a, b, (((1,), (1,)), ((), ())), preferred_element_type=F32)


def roll_z(v, step):
    if step == 0:
        return v
    parts = [
        pltpu.roll(v[:, k : k + 128], (-step) % 128, 1) for k in range(0, v.shape[1], 128)
    ]
    return parts[0] if len(parts) == 1 else jnp.concatenate(parts, axis=1)


def iota(shape, dim):
    return lax.broadcasted_iota(jnp.int32, shape, dim)


def select_matrix(rows, target):
    lanes = target.shape[1]
    return jnp.where(iota((rows, lanes), 0) == target, 1.0, 0.0).astype(BF16)


def taps_channels(y, t):
    lane = iota((1, 256), 1)
    b = (lane >> 6) - y
    c = (((lane >> 4) & 3) - t + 1) & 3
    ok = (b >= 0) & (b <= 2) & (c <= 2)
    return select_matrix(144, jnp.where(ok, b * 48 + c * 16 + (lane & 15), -1))


def taps_single(y, t):
    lane = iota((1, 144), 1)
    d = (lane >= 48).astype(jnp.int32) + (lane >= 96).astype(jnp.int32)
    b = ((lane >> 2) & 3) - y
    c = ((lane & 3) - t + 1) & 3
    ok = (b >= 0) & (b <= 2) & (c <= 2)
    return select_matrix(81, jnp.where(ok, ((lane >> 4) - 3 * d) * 27 + b * 9 + c * 3 + d, -1))


def taps_heads(y, t):
    lane = iota((1, 432), 1)
    group = sum((lane >= 48 * k).astype(jnp.int32) for k in range(1, 9))
    rest = lane - 48 * group
    b = 2 * (rest >> 4) + ((rest >> 2) & 1) - y - 1
    c = ((rest & 3) - t + 1) & 3
    ok = (b >= 0) & (b <= 2) & (c <= 2)
    target = group * 18 + ((rest >> 3) & 1) * 9 + b * 3 + c
    return select_matrix(162, jnp.where(ok, target, -1))


def split(v):
    high = v.astype(BF16)
    return high, (v - high.astype(F32)).astype(BF16)


def kernel(
    nx, ny, sites, noise_ref, wall_ref, w1_ref, w3t_ref, b1_ref, b2_ref, b3_ref,
    field_ref, ngrad_ref, pack_ref,
    win, inr, clw, clr, g2, g2t, g1, g3t, h1, h2, cm, cf, fld, partial_ref, parts, total,
    send_a, recv_a, send_b, recv_b, send_c, recv_c, send_d, recv_d,
):
    ix, iy = lax.axis_index("gx"), lax.axis_index("gy")
    devices = nx * ny
    me = ix * ny + iy

    def place(index):
        return (lax.div(index, ny), lax.rem(index, ny))

    def contribute(chunks):
        for c in chunks:
            @pl.when(me != c)
            def _():
                slot = lax.rem(me - c - 1 + devices, devices)
                pltpu.make_async_remote_copy(
                    src_ref=partial_ref.at[pl.ds(8 * c, 8)],
                    dst_ref=parts.at[pl.ds(pl.multiple_of(slot * 8, 8), 8)],
                    send_sem=send_c.at[c],
                    recv_sem=recv_c,
                    device_id=(c // ny, c % ny),
                    device_id_type=MESH,
                ).start()

    def peer(dx, dy):
        return (lax.rem(ix + dx + 2 * nx, nx), lax.rem(iy + dy + 2 * ny, ny))

    def exchange(ref, rows, send, recv):
        copies = []
        for k, (dx, dy) in enumerate(OFFSETS):
            copies.append(
                pltpu.make_async_remote_copy(
                    src_ref=ref.at[pl.ds(2 * rows, rows), pl.ds(512, 256)],
                    dst_ref=ref.at[pl.ds((2 - dy) * rows, rows), pl.ds((2 - dx) * 256, 256)],
                    send_sem=send.at[k],
                    recv_sem=recv.at[k],
                    device_id=peer(dx, dy),
                    device_id_type=MESH,
                )
            )
        return copies

    for x in range(2):
        for y in range(2):
            win[pl.ds(16 + 4 * y, 4), pl.ds(512 + 128 * x, 128)] = noise_ref[x, y]

    barrier = pltpu.get_barrier_semaphore()

    def greet(k, _):
        pl.semaphore_signal(
            barrier, inc=1, device_id=place(lax.rem(me + k, devices)), device_id_type=MESH
        )
        return 0

    lax.fori_loop(1, devices, greet, 0)
    pl.semaphore_wait(barrier, devices - 1)
    first = exchange(win, 8, send_a, recv_a)
    for copy in first:
        copy.start()

    wall = wall_ref[...]
    w1 = w1_ref[...]
    w3t = w3t_ref[...]
    small = []
    for n, (y, t) in enumerate(PAIRS):
        full = dot(wall, taps_channels(y, t)).astype(BF16)
        for a in range(3):
            for d in range(3):
                g2[a, pl.ds(d * 128 + n * 16, 16), :] = full[(3 * a + d) * 16 : (3 * a + d) * 16 + 16]
                g2t[a, pl.ds(d * 128 + n * 16, 16), :] = full[
                    144 + (3 * a + d) * 16 : 144 + (3 * a + d) * 16 + 16
                ]
        small.append(full[288:320])
        g1[pl.ds(n * 16, 16), :] = dot(w1, taps_single(y, t)).astype(BF16)
        g3t[pl.ds(n * 16, 16), :] = dot(w3t, taps_heads(y, t)).astype(BF16)
    small = jnp.concatenate(small, axis=0)
    row = iota((216, 256), 0)
    order = jnp.where((row & 7) * 32 + (row >> 3) == iota((216, 256), 1), 1.0, 0.0).astype(BF16)
    small = dot(order, small).astype(BF16)
    g3 = [small[48 * a : 48 * a + 48] for a in range(3)]
    g1t = [small[144 + 24 * a : 168 + 24 * a] for a in range(3)]
    b1, b2 = b1_ref[...], b2_ref[...]
    bias1 = jnp.concatenate([b1] * 8, axis=0)
    bias2 = jnp.concatenate([b2] * 8, axis=0)

    for copy in first:
        copy.wait()

    noise_all = win[...]
    parity = (iota((40, 1280), 0) >> 2) + iota((40, 1280), 0) + (iota((40, 1280), 1) >> 7) + iota((40, 1280), 1)
    inputs = jnp.where((parity & 1) == 0, noise_all, 0.0).astype(BF16).astype(F32)
    for d in range(3):
        inr[d] = roll_z(inputs, d - 1)
    for j in range(4):
        stack = jnp.concatenate(
            [
                inr[d, pl.ds(8 * j, 16), pl.ds(128 * a, 1024)]
                for d in range(3)
                for a in range(3)
            ],
            axis=0,
        ).astype(BF16)
        h1[pl.ds(128 * j, 128), :] = jnp.tanh(dot(g1[...], stack) + bias1).astype(BF16)

    def conv(mats, ref, start, width, rows):
        out = None
        for a in range(3):
            part = dot(mats[a], ref[pl.ds(start, 256), pl.ds(128 * a, width)])
            out = part if out is None else out + part
        total = out[rows : 2 * rows]
        for d in (0, 2):
            total = total + roll_z(out[d * rows : (d + 1) * rows], d - 1)
        return total

    for k in range(3):
        h2[pl.ds(128 * k, 128), :] = jnp.tanh(
            conv(g2, h1, 128 * k, 768, 128) + bias2
        ).astype(BF16)

    scales, growths = [], []
    for k in range(2):
        head = conv(g3, h2, 128 * k, 512, 16)
        log_scale = jnp.tanh(head[:8] + b3_ref[0])
        offset = head[8:] + b3_ref[1]
        noise = win[pl.ds(12 + 8 * k, 8), pl.ds(384, 512)]
        growth = jnp.exp(log_scale)
        r, l = iota((8, 512), 0), iota((8, 512), 1)
        even = (((r >> 2) + r + (l >> 7) + l) & 1) == 0
        fld[pl.ds(8 * k, 8), :] = jnp.where(even, noise, noise * growth + offset)
        scales.append(log_scale)
    log_scale = jnp.concatenate([scales[0][4:], scales[1][:4]], axis=0)[:, 128:384]
    growth = jnp.exp(log_scale)
    noise = win[pl.ds(16, 8), pl.ds(512, 256)]
    field = fld[pl.ds(4, 8), pl.ds(128, 256)]
    r, l = iota((8, 256), 0), iota((8, 256), 1)
    frozen = (((r >> 2) + r + (l >> 7) + l) & 1) == 0
    active = jnp.where(frozen, 0.0, 1.0)
    t_up = jnp.concatenate([field[1:4], field[0:1], field[5:8], field[4:5]], axis=0)
    t_down = jnp.concatenate([field[3:4], field[0:3], field[7:8], field[4:7]], axis=0)
    upward = (
        fld[pl.ds(4, 8), pl.ds(256, 256)] + fld[pl.ds(8, 8), pl.ds(128, 256)]
        + t_up + roll_z(field, 1)
    )
    downward = (
        fld[pl.ds(4, 8), pl.ds(0, 256)] + fld[pl.ds(0, 8), pl.ds(128, 256)]
        + t_down + roll_z(field, -1)
    )
    squared = field * field
    density = (
        -2.0 * HOPPING * field * upward + squared + QUARTIC * (squared - 1.0) * (squared - 1.0)
    )
    loss = jnp.sum(
        jnp.sum(-0.5 * noise * noise - active * log_scale + density, axis=1, keepdims=True),
        axis=0, keepdims=True,
    )
    force = (
        -2.0 * HOPPING * (upward + downward) + 2.0 * field + 4.0 * QUARTIC * field * (squared - 1.0)
    )
    d_scale = active * (force * noise * growth - 1.0) * (1.0 - log_scale * log_scale)
    d_offset = active * force
    cot_last = jnp.concatenate([d_scale, d_offset], axis=0).astype(BF16)
    clw[pl.ds(32, 16), pl.ds(512, 256)] = cot_last
    second = exchange(clw, 16, send_b, recv_b)
    for copy in second:
        copy.start()
    for x in range(2):
        for y in range(2):
            field_ref[x, y] = field[4 * y : 4 * y + 4, 128 * x : 128 * x + 128]

    cot_f = cot_last.astype(F32)
    bias_last = jnp.sum(cot_f, axis=1, keepdims=True)
    bias_last = jnp.concatenate(
        [jnp.sum(bias_last[:8], axis=0, keepdims=True), jnp.sum(bias_last[8:], axis=0, keepdims=True)],
        axis=0,
    )
    turned = jnp.concatenate([roll_z(cot_f, 1 - d) for d in range(3)], axis=0).astype(BF16)
    row, col = iota((64, 48), 0), iota((64, 48), 1)
    order = jnp.where((row & 7) * 8 + (row >> 3) == col, 1.0, 0.0).astype(BF16)
    turned = dot(order, turned).astype(BF16)
    last_products = [
        dot_nt(turned, h2[pl.ds(64, 256), pl.ds(128 * (a + 1), 256)]) for a in range(3)
    ]

    for copy in second:
        copy.wait()

    everywhere = clw[...].astype(F32)
    for d in range(3):
        clr[d] = roll_z(everywhere, d - 1).astype(BF16)
    for k in range(3):
        stack = jnp.concatenate(
            [
                clr[d, pl.ds(16 * k, 48), pl.ds(128 * (a + 1), 768)]
                for d in range(3)
                for a in range(3)
            ],
            axis=0,
        )
        hidden = h2[pl.ds(128 * k, 128), :].astype(F32)
        cm[pl.ds(128 * k, 128), :] = (dot(g3t[...], stack) * (1.0 - hidden * hidden)).astype(BF16)

    mine = cm[pl.ds(128, 128), pl.ds(256, 256)].astype(F32)
    bias_mid = jnp.sum(mine, axis=1, keepdims=True)
    bias_mid = sum(bias_mid[16 * n : 16 * n + 16] for n in range(8))
    turned = jnp.concatenate([roll_z(mine, 1 - d) for d in range(3)], axis=0).astype(BF16)
    products = [dot_nt(turned, h1[pl.ds(128, 256), pl.ds(128 * (a + 2), 256)]) for a in range(3)]
    folded = None
    for n, (y, t) in enumerate(PAIRS):
        piece = jnp.concatenate(
            [
                products[a][d * 128 + n * 16 : d * 128 + n * 16 + 16]
                for a in range(3)
                for d in range(3)
            ]
            + [last_products[a][8 * n : 8 * n + 8] for a in range(3)],
            axis=0,
        )
        high, low = split(piece)
        matrix = taps_channels(y, t)
        part = dot_nt(high, matrix) + dot_nt(low, matrix)
        folded = part if folded is None else folded + part
    partial_ref[pl.ds(0, 168), :] = folded[:, :128]
    partial_ref[pl.ds(184, 24), :] = jnp.concatenate(
        [folded[24 * q : 24 * q + 24, 128:] for q in range(7)] + [jnp.zeros((24, 16), F32)], axis=1
    )
    contribute([c for c in range(CHUNKS) if c not in (21, 22)])

    for k in range(2):
        hidden = h1[pl.ds(128 * (k + 1), 128), pl.ds(256, 512)].astype(F32)
        cf[pl.ds(128 * k, 128), :] = (
            conv(g2t, cm, 128 * k, 512, 128) * (1.0 - hidden * hidden)
        ).astype(BF16)
    mine = cf[pl.ds(64, 128), pl.ds(128, 256)]
    bias_first = jnp.sum(mine.astype(F32), axis=1, keepdims=True)
    bias_first = sum(bias_first[16 * n : 16 * n + 16] for n in range(8))
    stack = jnp.concatenate(
        [inr[d, pl.ds(12, 16), pl.ds(128 * (a + 3), 256)] for d in range(3) for a in range(3)], axis=0
    ).astype(BF16)
    product = dot_nt(mine, stack)
    folded = None
    for n, (y, t) in enumerate(PAIRS):
        high, low = split(product[16 * n : 16 * n + 16])
        matrix = taps_single(y, t)
        part = dot_nt(high, matrix) + dot_nt(low, matrix)
        folded = part if folded is None else folded + part
    pad = jnp.zeros((14, 1), F32)
    partial_ref[pl.ds(168, 16), :] = jnp.concatenate(
        [
            folded, bias_mid, bias_first, jnp.concatenate([bias_last, pad], axis=0),
            jnp.concatenate([loss, pad, jnp.zeros((1, 1), F32)], axis=0), jnp.zeros((16, 43), F32),
        ],
        axis=1,
    )
    contribute([21, 22])

    back = conv(g1t, cf, 0, 256, 8)
    result = jnp.where(frozen, back, 0.0) + force * jnp.where(frozen, 1.0, growth) - noise
    for x in range(2):
        for y in range(2):
            ngrad_ref[x, y] = result[4 * y : 4 * y + 4, 128 * x : 128 * x + 128]

    @pl.when(me < CHUNKS)
    def _():
        pltpu.make_async_copy(parts, parts, recv_c).wait()
        rows = pl.ds(pl.multiple_of(me * 8, 8), 8)
        summed = partial_ref[rows, :]
        for k in range(devices - 1):
            summed = summed + parts[pl.ds(8 * k, 8), :]
        total[rows, :] = summed / sites

        def share(k, _):
            pltpu.make_async_remote_copy(
                src_ref=total.at[rows],
                dst_ref=total.at[rows],
                send_sem=send_d,
                recv_sem=recv_d.at[me],
                device_id=place(lax.rem(me + k, devices)),
                device_id_type=MESH,
            ).start()
            return 0

        lax.fori_loop(1, devices, share, 0)

    for c in range(CHUNKS):
        @pl.when(me != c)
        def _():
            pltpu.make_async_copy(
                partial_ref.at[pl.ds(8 * c, 8)], partial_ref.at[pl.ds(8 * c, 8)], send_c.at[c]
            ).wait()
            pltpu.make_async_copy(
                total.at[pl.ds(8 * c, 8)], total.at[pl.ds(8 * c, 8)], recv_d.at[c]
            ).wait()

    pack_ref[...] = total[...]

    @pl.when(me < CHUNKS)
    def _():
        pltpu.make_async_copy(parts, parts, send_d).wait()


def unpack(
    pack_ref, field_ref, ngrad_ref,
    field_out, ngrad_out, loss_out, w1_out, b1_out, w2_out, b2_out, w3_out, b3_out,
):
    field_out[...] = field_ref[...]
    ngrad_out[...] = ngrad_ref[...]
    last_taps = pack_ref[pl.ds(184, 24), :]
    last_taps = jnp.concatenate(
        [last_taps[:, 16 * q : 16 * q + 16] for q in range(7)], axis=0
    )

    def taps(start, rows, g):
        if g == 8:
            return last_taps[start : start + rows]
        return pack_ref[pl.ds(start, rows), :][:, 16 * g : 16 * g + 16]

    for a in range(3):
        for g in range(9):
            heads = taps(144 + 8 * a, 8, g)
            for d in range(3):
                w2_out[a, g // 3, g % 3, d] = taps((3 * a + d) * 16, 16, g)
                w3_out[a, g // 3, g % 3, d] = heads[2 * d : 2 * d + 2]
    extra = jnp.transpose(pack_ref[pl.ds(168, 16), :], (1, 0))
    for r in range(81):
        w1_out[r // 27, (r // 9) % 3, (r // 3) % 3, r % 3] = extra[r : r + 1]
    b2_out[...] = extra[81:82]
    b1_out[...] = extra[82:83]
    b3_out[...] = extra[83:84, :2]
    loss_out[...] = extra[84:85, :1]


def local(nx, ny, noise, w_first, b_first, w_middle, b_middle, w_last, b_last):
    sites = float(noise.size * nx * ny)
    wm = jnp.transpose(w_middle, (2, 5, 0, 3, 4, 1)).reshape(144, 144)
    wmt = jnp.transpose(w_middle[:, :, ::-1, ::-1, ::-1, ::-1], (2, 5, 1, 3, 4, 0)).reshape(144, 144)
    wl = jnp.transpose(w_last, (2, 5, 0, 3, 4, 1)).reshape(18, 144)
    wft = jnp.transpose(w_first[:, 0, ::-1, ::-1, ::-1, ::-1], (1, 4, 2, 3, 0)).reshape(9, 144)
    wall = jnp.concatenate([wm, wmt, wl, wft, jnp.zeros((5, 144), BF16)], axis=0)
    w1 = w_first.reshape(16, 81)
    w3t = jnp.transpose(w_last[:, :, ::-1, ::-1, ::-1, ::-1], (1, 5, 2, 0, 3, 4)).reshape(16, 162)
    vmem = pl.BlockSpec(memory_space=pltpu.VMEM)
    smem = pl.BlockSpec(memory_space=pltpu.SMEM)
    devices = nx * ny
    field, ngrad, pack = pl.pallas_call(
        functools.partial(kernel, nx, ny, sites),
        out_shape=(
            jax.ShapeDtypeStruct(noise.shape, F32),
            jax.ShapeDtypeStruct(noise.shape, F32),
            jax.ShapeDtypeStruct((8 * CHUNKS, 128), F32),
        ),
        in_specs=[vmem] * 6 + [smem],
        out_specs=(vmem, vmem, vmem),
        scratch_shapes=[
            pltpu.VMEM((40, 1280), F32),
            pltpu.VMEM((3, 40, 1280), F32),
            pltpu.VMEM((80, 1280), BF16),
            pltpu.VMEM((3, 80, 1280), BF16),
            pltpu.VMEM((3, 384, 256), BF16),
            pltpu.VMEM((3, 384, 256), BF16),
            pltpu.VMEM((128, 144), BF16),
            pltpu.VMEM((128, 432), BF16),
            pltpu.VMEM((512, 1024), BF16),
            pltpu.VMEM((384, 768), BF16),
            pltpu.VMEM((384, 768), BF16),
            pltpu.VMEM((256, 512), BF16),
            pltpu.VMEM((16, 512), F32),
            pltpu.VMEM((8 * CHUNKS, 128), F32),
            pltpu.VMEM((8 * (devices - 1), 128), F32),
            pltpu.VMEM((8 * CHUNKS, 128), F32),
        ]
        + [pltpu.SemaphoreType.DMA((24,))] * 4
        + [pltpu.SemaphoreType.DMA((CHUNKS,)), pltpu.SemaphoreType.DMA] * 1
        + [pltpu.SemaphoreType.DMA, pltpu.SemaphoreType.DMA((CHUNKS,))],
        compiler_params=pltpu.CompilerParams(
            collective_id=0, has_side_effects=True, vmem_limit_bytes=32 * 1024 * 1024
        ),
    )(noise, wall, w1, w3t, b_first[:, None], b_middle[:, None], b_last)
    field, ngrad, loss, first, bias1, middle, bias2, last, bias3 = pl.pallas_call(
        unpack,
        out_shape=(
            jax.ShapeDtypeStruct(noise.shape, F32),
            jax.ShapeDtypeStruct(noise.shape, F32),
            jax.ShapeDtypeStruct((1, 1), F32),
            jax.ShapeDtypeStruct((3, 3, 3, 3, 1, 16), F32),
            jax.ShapeDtypeStruct((1, 16), F32),
            jax.ShapeDtypeStruct((3, 3, 3, 3, 16, 16), F32),
            jax.ShapeDtypeStruct((1, 16), F32),
            jax.ShapeDtypeStruct((3, 3, 3, 3, 2, 16), F32),
            jax.ShapeDtypeStruct((1, 2), F32),
        ),
        in_specs=[vmem] * 3,
        out_specs=(vmem,) * 9,
    )(pack, field, ngrad)
    order = (4, 5, 0, 1, 2, 3)
    return (
        field, ngrad, loss.reshape(()), jnp.transpose(first, (5, 4, 0, 1, 2, 3)),
        bias1.reshape(16), jnp.transpose(middle, order), bias2.reshape(16),
        jnp.transpose(last, order), bias3.reshape(2),
    )


def solution(mesh):
    placed = (P("gx", "gy", None, None), P(), P(), P(), P(), P(), P())
    return jax.shard_map(
        functools.partial(local, mesh.shape["gx"], mesh.shape["gy"]),
        mesh=mesh,
        in_specs=placed,
        out_specs=(
            P("gx", "gy", None, None), P("gx", "gy", None, None), P(), P(), P(), P(), P(), P(), P(),
        ),
        check_vma=False,
    )
```

```python
import functools

import jax
import jax.numpy as jnp
from jax import lax
from jax.experimental import pallas as pl
from jax.experimental.pallas import tpu as pltpu
from jax.sharding import PartitionSpec as P

HOPPING = 0.15
QUARTIC = 0.1
MESH = pl.DeviceIdType.MESH
F32 = jnp.float32
BF16 = jnp.bfloat16
OFFSETS = [(dx, dy) for dx in range(-2, 3) for dy in range(-2, 3) if (dx, dy) != (0, 0)]
CHUNKS = 12
PAIRS = [(y, t) for y in range(2) for t in range(4)]


def dot(a, b):
    return jnp.dot(a, b, preferred_element_type=F32)


def dot_nt(a, b):
    return lax.dot_general(a, b, (((1,), (1,)), ((), ())), preferred_element_type=F32)


def roll_z(v, step):
    if step == 0:
        return v
    parts = [
        pltpu.roll(v[:, k : k + 128], (-step) % 128, 1) for k in range(0, v.shape[1], 128)
    ]
    return parts[0] if len(parts) == 1 else jnp.concatenate(parts, axis=1)


def iota(shape, dim):
    return lax.broadcasted_iota(jnp.int32, shape, dim)


def select_matrix(rows, target):
    lanes = target.shape[1]
    return jnp.where(iota((rows, lanes), 0) == target, 1.0, 0.0).astype(BF16)


def taps_channels(y, t):
    lane = iota((1, 256), 1)
    b = (lane >> 6) - y
    c = (((lane >> 4) & 3) - t + 1) & 3
    ok = (b >= 0) & (b <= 2) & (c <= 2)
    return select_matrix(144, jnp.where(ok, b * 48 + c * 16 + (lane & 15), -1))


def taps_single(y, t):
    lane = iota((1, 144), 1)
    d = (lane >= 48).astype(jnp.int32) + (lane >= 96).astype(jnp.int32)
    b = ((lane >> 2) & 3) - y
    c = ((lane & 3) - t + 1) & 3
    ok = (b >= 0) & (b <= 2) & (c <= 2)
    return select_matrix(81, jnp.where(ok, ((lane >> 4) - 3 * d) * 27 + b * 9 + c * 3 + d, -1))


def taps_heads(y, t):
    lane = iota((1, 432), 1)
    group = sum((lane >= 48 * k).astype(jnp.int32) for k in range(1, 9))
    rest = lane - 48 * group
    b = 2 * (rest >> 4) + ((rest >> 2) & 1) - y - 1
    c = ((rest & 3) - t + 1) & 3
    ok = (b >= 0) & (b <= 2) & (c <= 2)
    target = group * 18 + ((rest >> 3) & 1) * 9 + b * 3 + c
    return select_matrix(162, jnp.where(ok, target, -1))


def split(v):
    high = v.astype(BF16)
    return high, (v - high.astype(F32)).astype(BF16)


def kernel(
    nx, ny, sites, noise_ref, wall_ref, w1_ref, w3t_ref, b1_ref, b2_ref, b3_ref,
    pack_ref,
    win, inr, clw, clr, g2, g2t, g1, g3t, h1, h2, cm, cf, fld, tp,
    partial_ref, parts, total, extra_ref, extra_parts, extra_total,
    send_a, recv_a, send_b, recv_b, send_c, recv_c, recv_d, send_d, recv_e, send_f,
):
    ix, iy = lax.axis_index("gx"), lax.axis_index("gy")
    devices = nx * ny
    me = ix * ny + iy

    def place(index):
        return (lax.div(index, ny), lax.rem(index, ny))

    def owner(c):
        return c * devices // (CHUNKS + 1)

    def contribute(c, source, buffer, arrived):
        @pl.when(me != owner(c))
        def _():
            slot = lax.rem(me - owner(c) - 1 + devices, devices)
            pltpu.make_async_remote_copy(
                src_ref=source,
                dst_ref=buffer.at[pl.ds(pl.multiple_of(slot * 16, 16), 16)],
                send_sem=send_c.at[c],
                recv_sem=arrived,
                device_id=(owner(c) // ny, owner(c) % ny),
                device_id_type=MESH,
            ).start()

    def share(c, ref, sent):
        def step(k, _):
            pltpu.make_async_remote_copy(
                src_ref=ref,
                dst_ref=ref,
                send_sem=sent,
                recv_sem=recv_d.at[c],
                device_id=place(lax.rem(me + k, devices)),
                device_id_type=MESH,
            ).start()
            return 0

        lax.fori_loop(1, devices, step, 0)

    def peer(dx, dy):
        return (lax.rem(ix + dx + 2 * nx, nx), lax.rem(iy + dy + 2 * ny, ny))

    def exchange(ref, rows, send, recv):
        copies = []
        for k, (dx, dy) in enumerate(OFFSETS):
            if dx == 2 and nx == 4:
                continue
            copies.append(
                pltpu.make_async_remote_copy(
                    src_ref=ref.at[pl.ds(2 * rows, rows), pl.ds(512, 256)],
                    dst_ref=ref.at[pl.ds((2 - dy) * rows, rows), pl.ds((2 - dx) * 256, 256)],
                    send_sem=send.at[k],
                    recv_sem=recv.at[k],
                    device_id=peer(dx, dy),
                    device_id_type=MESH,
                )
            )
        return copies

    for x in range(2):
        for y in range(2):
            win[pl.ds(16 + 4 * y, 4), pl.ds(512 + 128 * x, 128)] = noise_ref[x, y]

    barrier = pltpu.get_barrier_semaphore()

    def greet(k, _):
        pl.semaphore_signal(
            barrier, inc=1, device_id=place(lax.rem(me + k, devices)), device_id_type=MESH
        )
        return 0

    lax.fori_loop(1, devices, greet, 0)
    pl.semaphore_wait(barrier, devices - 1)
    first = exchange(win, 8, send_a, recv_a)
    for copy in first:
        copy.start()

    wall = wall_ref[...]
    w1 = w1_ref[...]
    w3t = w3t_ref[...]
    small = []
    for n, (y, t) in enumerate(PAIRS):
        matrix = taps_channels(y, t)
        tp[:, pl.ds(256 * n, 256)] = matrix
        full = dot(wall, matrix).astype(BF16)
        for a in range(3):
            for d in range(3):
                where = (pl.ds(d * 128 + n * 16, 16), pl.ds(256 * a, 256))
                g2[where] = full[(3 * a + d) * 16 : (3 * a + d) * 16 + 16]
                g2t[where] = full[
                    144 + (3 * a + d) * 16 : 144 + (3 * a + d) * 16 + 16
                ]
        small.append(full[288:320])
        g1[pl.ds(n * 16, 16), :] = dot(w1, taps_single(y, t)).astype(BF16)
        g3t[pl.ds(n * 16, 16), :] = dot(w3t, taps_heads(y, t)).astype(BF16)
    small = jnp.concatenate(small, axis=0)
    row = iota((216, 256), 0)
    order = jnp.where((row & 7) * 32 + (row >> 3) == iota((216, 256), 1), 1.0, 0.0).astype(BF16)
    small = dot(order, small).astype(BF16)
    g3 = jnp.concatenate([small[48 * a : 48 * a + 48] for a in range(3)], axis=1)
    g1t = jnp.concatenate([small[144 + 24 * a : 168 + 24 * a] for a in range(3)], axis=1)
    b1, b2 = b1_ref[...], b2_ref[...]
    bias1 = jnp.concatenate([b1] * 8, axis=0)
    bias2 = jnp.concatenate([b2] * 8, axis=0)

    for copy in first:
        copy.wait()
    if nx == 4:
        win[:, pl.ds(0, 256)] = win[:, pl.ds(1024, 256)]

    noise_all = win[...]
    parity = (iota((40, 1280), 0) >> 2) + iota((40, 1280), 0) + (iota((40, 1280), 1) >> 7) + iota((40, 1280), 1)
    inputs = jnp.where((parity & 1) == 0, noise_all, 0.0).astype(BF16).astype(F32)
    for d in range(3):
        inr[d] = roll_z(inputs, d - 1)
    for j in range(4):
        stack = jnp.concatenate(
            [
                inr[d, pl.ds(8 * j, 16), pl.ds(128 * a, 1024)]
                for d in range(3)
                for a in range(3)
            ],
            axis=0,
        ).astype(BF16)
        h1[pl.ds(128 * j, 128), :] = jnp.tanh(dot(g1[...], stack) + bias1).astype(BF16)

    def conv(mats, ref, start, width, rows):
        stack = [ref[pl.ds(start, 256), pl.ds(128 * a, width)] for a in range(3)]
        out = dot(mats[...], jnp.concatenate(stack, axis=0))
        total = out[rows : 2 * rows]
        for d in (0, 2):
            total = total + roll_z(out[d * rows : (d + 1) * rows], d - 1)
        return total

    for k in range(3):
        h2[pl.ds(128 * k, 128), :] = jnp.tanh(
            conv(g2, h1, 128 * k, 768, 128) + bias2
        ).astype(BF16)

    scales, growths = [], []
    for k in range(2):
        head = conv(g3, h2, 128 * k, 512, 16)
        log_scale = jnp.tanh(head[:8] + b3_ref[0])
        offset = head[8:] + b3_ref[1]
        noise = win[pl.ds(12 + 8 * k, 8), pl.ds(384, 512)]
        growth = jnp.exp(log_scale)
        r, l = iota((8, 512), 0), iota((8, 512), 1)
        even = (((r >> 2) + r + (l >> 7) + l) & 1) == 0
        fld[pl.ds(8 * k, 8), :] = jnp.where(even, noise, noise * growth + offset)
        scales.append(log_scale)
    log_scale = jnp.concatenate([scales[0][4:], scales[1][:4]], axis=0)[:, 128:384]
    growth = jnp.exp(log_scale)
    noise = win[pl.ds(16, 8), pl.ds(512, 256)]
    field = fld[pl.ds(4, 8), pl.ds(128, 256)]
    r, l = iota((8, 256), 0), iota((8, 256), 1)
    frozen = (((r >> 2) + r + (l >> 7) + l) & 1) == 0
    active = jnp.where(frozen, 0.0, 1.0)
    t_up = jnp.concatenate([field[1:4], field[0:1], field[5:8], field[4:5]], axis=0)
    t_down = jnp.concatenate([field[3:4], field[0:3], field[7:8], field[4:7]], axis=0)
    upward = (
        fld[pl.ds(4, 8), pl.ds(256, 256)] + fld[pl.ds(8, 8), pl.ds(128, 256)]
        + t_up + roll_z(field, 1)
    )
    downward = (
        fld[pl.ds(4, 8), pl.ds(0, 256)] + fld[pl.ds(0, 8), pl.ds(128, 256)]
        + t_down + roll_z(field, -1)
    )
    squared = field * field
    density = (
        -2.0 * HOPPING * field * upward + squared + QUARTIC * (squared - 1.0) * (squared - 1.0)
    )
    loss = jnp.sum(
        jnp.sum(-0.5 * noise * noise - active * log_scale + density, axis=1, keepdims=True),
        axis=0, keepdims=True,
    )
    force = (
        -2.0 * HOPPING * (upward + downward) + 2.0 * field + 4.0 * QUARTIC * field * (squared - 1.0)
    )
    d_scale = active * (force * noise * growth - 1.0) * (1.0 - log_scale * log_scale)
    d_offset = active * force
    cot_last = jnp.concatenate([d_scale, d_offset], axis=0).astype(BF16)
    clw[pl.ds(32, 16), pl.ds(512, 256)] = cot_last
    second = exchange(clw, 16, send_b, recv_b)
    for copy in second:
        copy.start()
    for x in range(2):
        for y in range(2):
            pack_ref[pl.ds(208 + 8 * x + 4 * y, 4), :] = field[4 * y : 4 * y + 4, 128 * x : 128 * x + 128]

    cot_f = cot_last.astype(F32)
    bias_last = jnp.sum(cot_f, axis=1, keepdims=True)
    bias_last = jnp.concatenate(
        [jnp.sum(bias_last[:8], axis=0, keepdims=True), jnp.sum(bias_last[8:], axis=0, keepdims=True)],
        axis=0,
    )
    turned = jnp.concatenate([roll_z(cot_f, 1 - d) for d in range(3)], axis=0).astype(BF16)
    row, col = iota((64, 48), 0), iota((64, 48), 1)
    order = jnp.where((row & 7) * 8 + (row >> 3) == col, 1.0, 0.0).astype(BF16)
    turned = dot(order, turned).astype(BF16)
    last_products = [
        dot_nt(turned, h2[pl.ds(64, 256), pl.ds(128 * (a + 1), 256)]) for a in range(3)
    ]

    for copy in second:
        copy.wait()
    if nx == 4:
        clw[:, pl.ds(0, 256)] = clw[:, pl.ds(1024, 256)]

    everywhere = clw[...].astype(F32)
    for d in range(3):
        clr[d] = roll_z(everywhere, d - 1).astype(BF16)
    for k in range(3):
        stack = jnp.concatenate(
            [
                clr[d, pl.ds(16 * k, 48), pl.ds(128 * (a + 1), 768)]
                for d in range(3)
                for a in range(3)
            ],
            axis=0,
        )
        hidden = h2[pl.ds(128 * k, 128), :].astype(F32)
        cm[pl.ds(128 * k, 128), :] = (dot(g3t[...], stack) * (1.0 - hidden * hidden)).astype(BF16)

    mine = cm[pl.ds(128, 128), pl.ds(256, 256)].astype(F32)
    bias_mid = jnp.sum(mine, axis=1, keepdims=True)
    bias_mid = sum(bias_mid[16 * n : 16 * n + 16] for n in range(8))
    turned = jnp.concatenate([roll_z(mine, 1 - d) for d in range(3)], axis=0).astype(BF16)
    products = [dot_nt(turned, h1[pl.ds(128, 256), pl.ds(128 * (a + 2), 256)]) for a in range(3)]
    pieces = []
    for n in range(8):
        pieces.append(
            jnp.concatenate(
                [
                    products[a][d * 128 + n * 16 : d * 128 + n * 16 + 16]
                    for a in range(3)
                    for d in range(3)
                ]
                + [last_products[a][8 * n : 8 * n + 8] for a in range(3)],
                axis=0,
            )
        )
    high, low = split(jnp.concatenate(pieces, axis=1))
    folded = dot_nt(high, tp[...]) + dot_nt(low, tp[...])
    partial_ref[pl.ds(0, 144), :] = folded[:144, :128].astype(BF16)
    partial_ref[pl.ds(144, 48), :] = jnp.concatenate(
        [
            folded[144:, :128],
            jnp.concatenate(
                [folded[24 * q : 24 * q + 24, 128:] for q in range(7)] + [jnp.zeros((24, 16), F32)],
                axis=1,
            ),
        ],
        axis=0,
    ).astype(BF16)
    for c in range(CHUNKS):
        contribute(c, partial_ref.at[pl.ds(16 * c, 16)], parts, recv_c)

    for k in range(2):
        hidden = h1[pl.ds(128 * (k + 1), 128), pl.ds(256, 512)].astype(F32)
        cf[pl.ds(128 * k, 128), :] = (
            conv(g2t, cm, 128 * k, 512, 128) * (1.0 - hidden * hidden)
        ).astype(BF16)
    mine = cf[pl.ds(64, 128), pl.ds(128, 256)]
    bias_first = jnp.sum(mine.astype(F32), axis=1, keepdims=True)
    bias_first = sum(bias_first[16 * n : 16 * n + 16] for n in range(8))
    stack = jnp.concatenate(
        [inr[d, pl.ds(12, 16), pl.ds(128 * (a + 3), 256)] for d in range(3) for a in range(3)], axis=0
    ).astype(BF16)
    product = dot_nt(mine, stack)
    folded = None
    for n, (y, t) in enumerate(PAIRS):
        high, low = split(product[16 * n : 16 * n + 16])
        matrix = taps_single(y, t)
        part = dot_nt(high, matrix) + dot_nt(low, matrix)
        folded = part if folded is None else folded + part
    pad = jnp.zeros((14, 1), F32)
    extra_ref[...] = jnp.concatenate(
        [
            folded, bias_mid, bias_first, jnp.concatenate([bias_last, pad], axis=0),
            jnp.concatenate([loss, pad, jnp.zeros((1, 1), F32)], axis=0), jnp.zeros((16, 43), F32),
        ],
        axis=1,
    )
    contribute(CHUNKS, extra_ref, extra_parts, recv_e)

    back = conv(g1t, cf, 0, 256, 8)
    result = jnp.where(frozen, back, 0.0) + force * jnp.where(frozen, 1.0, growth) - noise
    for x in range(2):
        for y in range(2):
            pack_ref[pl.ds(224 + 8 * x + 4 * y, 4), :] = result[4 * y : 4 * y + 4, 128 * x : 128 * x + 128]

    def add_up(own, buffer, result):
        summed = own.astype(F32)
        for k in range(devices - 1):
            summed = summed + buffer[pl.ds(16 * k, 16), :].astype(F32)
        return (summed / sites).astype(result)

    chunk = lax.div(me * (CHUNKS + 1) + devices - 1, devices)
    owns = (lax.div(chunk * devices, CHUNKS + 1) == me) & (chunk < CHUNKS)
    owns_extra = me == owner(CHUNKS)

    @pl.when(owns)
    def _():
        pltpu.make_async_copy(parts, parts, recv_c).wait()
        rows = pl.ds(pl.multiple_of(chunk * 16, 16), 16)
        total[rows, :] = add_up(partial_ref[rows, :], parts, BF16)
        share(chunk, total.at[rows], send_d)

    @pl.when(owns_extra)
    def _():
        pltpu.make_async_copy(extra_parts, extra_parts, recv_e).wait()
        extra_total[...] = add_up(extra_ref[...], extra_parts, F32)
        share(CHUNKS, extra_total, send_f)

    for c in range(CHUNKS + 1):
        @pl.when(me != owner(c))
        def _():
            sent = extra_ref if c == CHUNKS else partial_ref.at[pl.ds(16 * c, 16)]
            given = extra_total if c == CHUNKS else total.at[pl.ds(16 * c, 16)]
            pltpu.make_async_copy(sent, sent, send_c.at[c]).wait()
            pltpu.make_async_copy(given, given, recv_d.at[c]).wait()

    pack_ref[pl.ds(0, 192), :] = total[...].astype(F32)
    pack_ref[pl.ds(192, 16), :] = extra_total[...]

    @pl.when(owns)
    def _():
        pltpu.make_async_copy(parts, parts, send_d).wait()

    @pl.when(owns_extra)
    def _():
        pltpu.make_async_copy(extra_parts, extra_parts, send_f).wait()


def unpack(
    pack_ref,
    field_out, ngrad_out, loss_out, w1_out, b1_out, w2_out, b2_out, w3_out, b3_out,
):
    for x in range(2):
        for y in range(2):
            field_out[x, y] = pack_ref[pl.ds(208 + 8 * x + 4 * y, 4), :]
            ngrad_out[x, y] = pack_ref[pl.ds(224 + 8 * x + 4 * y, 4), :]
    last_taps = pack_ref[pl.ds(168, 24), :]
    last_taps = jnp.concatenate(
        [last_taps[:, 16 * q : 16 * q + 16] for q in range(7)], axis=0
    )

    def taps(start, rows, g):
        if g == 8:
            return last_taps[start : start + rows]
        return pack_ref[pl.ds(start, rows), :][:, 16 * g : 16 * g + 16]

    for a in range(3):
        for g in range(9):
            heads = taps(144 + 8 * a, 8, g)
            for d in range(3):
                w2_out[a, g // 3, g % 3, d] = taps((3 * a + d) * 16, 16, g)
                w3_out[a, g // 3, g % 3, d] = heads[2 * d : 2 * d + 2]
    extra = jnp.transpose(pack_ref[pl.ds(192, 16), :], (1, 0))
    for r in range(81):
        w1_out[r // 27, (r // 9) % 3, (r // 3) % 3, r % 3] = extra[r : r + 1]
    b2_out[...] = extra[81:82]
    b1_out[...] = extra[82:83]
    b3_out[...] = extra[83:84, :2]
    loss_out[...] = extra[84:85, :1]


def local(nx, ny, noise, w_first, b_first, w_middle, b_middle, w_last, b_last):
    sites = float(noise.size * nx * ny)
    wm = jnp.transpose(w_middle, (2, 5, 0, 3, 4, 1)).reshape(144, 144)
    wmt = jnp.transpose(w_middle[:, :, ::-1, ::-1, ::-1, ::-1], (2, 5, 1, 3, 4, 0)).reshape(144, 144)
    wl = jnp.transpose(w_last, (2, 5, 0, 3, 4, 1)).reshape(18, 144)
    wft = jnp.transpose(w_first[:, 0, ::-1, ::-1, ::-1, ::-1], (1, 4, 2, 3, 0)).reshape(9, 144)
    wall = jnp.concatenate([wm, wmt, wl, wft, jnp.zeros((5, 144), BF16)], axis=0)
    w1 = w_first.reshape(16, 81)
    w3t = jnp.transpose(w_last[:, :, ::-1, ::-1, ::-1, ::-1], (1, 5, 2, 0, 3, 4)).reshape(16, 162)
    vmem = pl.BlockSpec(memory_space=pltpu.VMEM)
    smem = pl.BlockSpec(memory_space=pltpu.SMEM)
    devices = nx * ny
    pack = pl.pallas_call(
        functools.partial(kernel, nx, ny, sites),
        out_shape=jax.ShapeDtypeStruct((240, 128), F32),
        in_specs=[vmem] * 6 + [smem],
        out_specs=vmem,
        scratch_shapes=[
            pltpu.VMEM((40, 1280), F32),
            pltpu.VMEM((3, 40, 1280), F32),
            pltpu.VMEM((80, 1280), BF16),
            pltpu.VMEM((3, 80, 1280), BF16),
            pltpu.VMEM((384, 768), BF16),
            pltpu.VMEM((384, 768), BF16),
            pltpu.VMEM((128, 144), BF16),
            pltpu.VMEM((128, 432), BF16),
            pltpu.VMEM((512, 1024), BF16),
            pltpu.VMEM((384, 768), BF16),
            pltpu.VMEM((384, 768), BF16),
            pltpu.VMEM((256, 512), BF16),
            pltpu.VMEM((16, 512), F32),
            pltpu.VMEM((144, 2048), BF16),
            pltpu.VMEM((16 * CHUNKS, 128), BF16),
            pltpu.VMEM((16 * (devices - 1), 128), BF16),
            pltpu.VMEM((16 * CHUNKS, 128), BF16),
            pltpu.VMEM((16, 128), F32),
            pltpu.VMEM((16 * (devices - 1), 128), F32),
            pltpu.VMEM((16, 128), F32),
        ]
        + [pltpu.SemaphoreType.DMA((24,))] * 4
        + [pltpu.SemaphoreType.DMA((CHUNKS + 1,)), pltpu.SemaphoreType.DMA] * 2
        + [pltpu.SemaphoreType.DMA] * 2,
        compiler_params=pltpu.CompilerParams(
            collective_id=0, has_side_effects=True, vmem_limit_bytes=32 * 1024 * 1024
        ),
    )(noise, wall, w1, w3t, b_first[:, None], b_middle[:, None], b_last)
    field, ngrad, loss, first, bias1, middle, bias2, last, bias3 = pl.pallas_call(
        unpack,
        out_shape=(
            jax.ShapeDtypeStruct(noise.shape, F32),
            jax.ShapeDtypeStruct(noise.shape, F32),
            jax.ShapeDtypeStruct((1, 1), F32),
            jax.ShapeDtypeStruct((3, 3, 3, 3, 1, 16), F32),
            jax.ShapeDtypeStruct((1, 16), F32),
            jax.ShapeDtypeStruct((3, 3, 3, 3, 16, 16), F32),
            jax.ShapeDtypeStruct((1, 16), F32),
            jax.ShapeDtypeStruct((3, 3, 3, 3, 2, 16), F32),
            jax.ShapeDtypeStruct((1, 2), F32),
        ),
        in_specs=[vmem],
        out_specs=(vmem,) * 9,
    )(pack)
    order = (4, 5, 0, 1, 2, 3)
    return (
        field, ngrad, loss.reshape(()), jnp.transpose(first, (5, 4, 0, 1, 2, 3)),
        bias1.reshape(16), jnp.transpose(middle, order), bias2.reshape(16),
        jnp.transpose(last, order), bias3.reshape(2),
    )


def solution(mesh):
    placed = (P("gx", "gy", None, None), P(), P(), P(), P(), P(), P())
    return jax.shard_map(
        functools.partial(local, mesh.shape["gx"], mesh.shape["gy"]),
        mesh=mesh,
        in_specs=placed,
        out_specs=(
            P("gx", "gy", None, None), P("gx", "gy", None, None), P(), P(), P(), P(), P(), P(), P(),
        ),
        check_vma=False,
    )
```

```python
import functools

import jax
import jax.numpy as jnp
from jax import lax
from jax.experimental import pallas as pl
from jax.experimental.pallas import tpu as pltpu
from jax.sharding import PartitionSpec as P

HOPPING = 0.15
QUARTIC = 0.1
MESH = pl.DeviceIdType.MESH
F32 = jnp.float32
BF16 = jnp.bfloat16
OFFSETS = [(dx, dy) for dx in range(-2, 3) for dy in range(-2, 3) if (dx, dy) != (0, 0)]
CHUNKS = 12
PAIRS = [(y, t) for y in range(2) for t in range(4)]


def dot(a, b):
    return jnp.dot(a, b, preferred_element_type=F32)


def dot_nt(a, b):
    return lax.dot_general(a, b, (((1,), (1,)), ((), ())), preferred_element_type=F32)


def roll_z(v, step):
    if step == 0:
        return v
    parts = [
        pltpu.roll(v[:, k : k + 128], (-step) % 128, 1) for k in range(0, v.shape[1], 128)
    ]
    return parts[0] if len(parts) == 1 else jnp.concatenate(parts, axis=1)


def iota(shape, dim):
    return lax.broadcasted_iota(jnp.int32, shape, dim)


def select_matrix(rows, target):
    lanes = target.shape[1]
    return jnp.where(iota((rows, lanes), 0) == target, 1.0, 0.0).astype(BF16)


def taps_channels(y, t):
    lane = iota((1, 256), 1)
    b = (lane >> 6) - y
    c = (((lane >> 4) & 3) - t + 1) & 3
    ok = (b >= 0) & (b <= 2) & (c <= 2)
    return select_matrix(144, jnp.where(ok, b * 48 + c * 16 + (lane & 15), -1))


def taps_single(y, t):
    lane = iota((1, 144), 1)
    d = (lane >= 48).astype(jnp.int32) + (lane >= 96).astype(jnp.int32)
    b = ((lane >> 2) & 3) - y
    c = ((lane & 3) - t + 1) & 3
    ok = (b >= 0) & (b <= 2) & (c <= 2)
    return select_matrix(81, jnp.where(ok, ((lane >> 4) - 3 * d) * 27 + b * 9 + c * 3 + d, -1))


def taps_heads(y, t):
    lane = iota((1, 432), 1)
    group = sum((lane >= 48 * k).astype(jnp.int32) for k in range(1, 9))
    rest = lane - 48 * group
    b = 2 * (rest >> 4) + ((rest >> 2) & 1) - y - 1
    c = ((rest & 3) - t + 1) & 3
    ok = (b >= 0) & (b <= 2) & (c <= 2)
    target = group * 18 + b * 6 + c * 2 + ((rest >> 3) & 1)
    return select_matrix(162, jnp.where(ok, target, -1))


def split(v):
    high = v.astype(BF16)
    return high, (v - high.astype(F32)).astype(BF16)


def kernel(
    nx, ny, sites, noise_hbm, w1_hbm, b1_hbm, w2_hbm, b2_hbm, w3_hbm, b3_hbm,
    pack_ref,
    noise_ref, w1_ref, b1_ref, w2_ref, b2_ref, w3_ref, b3_ref, wall_ref, w1_rows, w3_rows,
    win, inr, clw, clr, g2, g2t, g1, g3t, h1, h2, cm, cf, fld, tp,
    partial_ref, parts, total, extra_ref, extra_parts, extra_total,
    send_a, recv_a, send_b, recv_b, send_c, recv_c, recv_d, send_d, recv_e, send_f, load,
):
    ix, iy = lax.axis_index("gx"), lax.axis_index("gy")
    devices = nx * ny
    me = ix * ny + iy

    def place(index):
        return (lax.div(index, ny), lax.rem(index, ny))

    def owner(c):
        return c * devices // (CHUNKS + 1)

    def contribute(c, source, buffer, arrived):
        @pl.when(me != owner(c))
        def _():
            slot = lax.rem(me - owner(c) - 1 + devices, devices)
            pltpu.make_async_remote_copy(
                src_ref=source,
                dst_ref=buffer.at[pl.ds(pl.multiple_of(slot * 16, 16), 16)],
                send_sem=send_c.at[c],
                recv_sem=arrived,
                device_id=(owner(c) // ny, owner(c) % ny),
                device_id_type=MESH,
            ).start()

    def share(c, ref, sent):
        def step(k, _):
            pltpu.make_async_remote_copy(
                src_ref=ref,
                dst_ref=ref,
                send_sem=sent,
                recv_sem=recv_d.at[c],
                device_id=place(lax.rem(me + k, devices)),
                device_id_type=MESH,
            ).start()
            return 0

        lax.fori_loop(1, devices, step, 0)

    def peer(dx, dy):
        return (lax.rem(ix + dx + 2 * nx, nx), lax.rem(iy + dy + 2 * ny, ny))

    def exchange(ref, rows, send, recv):
        copies = []
        for k, (dx, dy) in enumerate(OFFSETS):
            if dx == 2 and nx == 4:
                continue
            copies.append(
                pltpu.make_async_remote_copy(
                    src_ref=ref.at[pl.ds(2 * rows, rows), pl.ds(512, 256)],
                    dst_ref=ref.at[pl.ds((2 - dy) * rows, rows), pl.ds((2 - dx) * 256, 256)],
                    send_sem=send.at[k],
                    recv_sem=recv.at[k],
                    device_id=peer(dx, dy),
                    device_id_type=MESH,
                )
            )
        return copies

    loads = [
        pltpu.make_async_copy(source, target, load.at[k])
        for k, (source, target) in enumerate(
            [
                (noise_hbm, noise_ref), (w1_hbm, w1_ref), (b1_hbm, b1_ref), (w2_hbm, w2_ref),
                (b2_hbm, b2_ref), (w3_hbm, w3_ref), (b3_hbm, b3_ref),
            ]
        )
    ]
    for copy in loads:
        copy.start()
    barrier = pltpu.get_barrier_semaphore()

    def greet(k, _):
        pl.semaphore_signal(
            barrier, inc=1, device_id=place(lax.rem(me + k, devices)), device_id_type=MESH
        )
        return 0

    lax.fori_loop(1, devices, greet, 0)
    loads[0].wait()
    for x in range(2):
        for y in range(2):
            win[pl.ds(16 + 4 * y, 4), pl.ds(512 + 128 * x, 128)] = noise_ref[x, y]
    pl.semaphore_wait(barrier, devices - 1)
    first = exchange(win, 8, send_a, recv_a)
    for copy in first:
        copy.start()

    for copy in loads[1:]:
        copy.wait()
    wall_ref[pl.ds(304, 16), :] = jnp.zeros((16, 144), F32)
    for a in range(3):
        for d in range(3):
            slabs = [w2_ref[a, g // 3, g % 3, d].astype(F32) for g in range(9)]
            wall_ref[pl.ds(16 * (3 * a + d), 16), :] = jnp.concatenate(slabs, axis=1)
            turned = jnp.transpose(jnp.concatenate(slabs[::-1], axis=0), (1, 0))
            wall_ref[pl.ds(144 + 16 * (3 * (2 - a) + 2 - d), 16), :] = turned
            heads = [w3_ref[a, g // 3, g % 3, d].astype(F32) for g in range(9)]
            wall_ref[pl.ds(288 + 2 * (3 * a + d), 2), :] = jnp.concatenate(heads, axis=1)
            for g in range(9):
                w3_rows[pl.ds((3 * (2 - d) + 2 - a) * 18 + 2 * (8 - g), 2), :] = heads[g]
        for g in range(9):
            row = w1_ref[0, a, g // 3, g % 3].astype(F32)
            w1_rows[pl.ds(27 * a + 3 * g, 3), :] = row
            wall_ref[pl.ds(306 + 3 * (2 - a), 3), pl.ds(16 * (8 - g), 16)] = row
    wall = wall_ref[...].astype(BF16)
    w1 = jnp.transpose(w1_rows[...], (1, 0))[:, :81].astype(BF16)
    w3t = jnp.transpose(w3_rows[...], (1, 0))[:, :162].astype(BF16)
    small = []
    for n, (y, t) in enumerate(PAIRS):
        matrix = taps_channels(y, t)
        tp[:, pl.ds(256 * n, 256)] = matrix
        full = dot(wall, matrix).astype(BF16)
        for a in range(3):
            for d in range(3):
                where = (pl.ds(d * 128 + n * 16, 16), pl.ds(256 * a, 256))
                g2[where] = full[(3 * a + d) * 16 : (3 * a + d) * 16 + 16]
                g2t[where] = full[
                    144 + (3 * a + d) * 16 : 144 + (3 * a + d) * 16 + 16
                ]
        small.append(full[288:320])
        g1[pl.ds(n * 16, 16), :] = dot(w1, taps_single(y, t)).astype(BF16)
        g3t[pl.ds(n * 16, 16), :] = dot(w3t, taps_heads(y, t)).astype(BF16)
    small = jnp.concatenate(small, axis=0)
    row = iota((216, 256), 0)
    order = jnp.where((row & 7) * 32 + (row >> 3) == iota((216, 256), 1), 1.0, 0.0).astype(BF16)
    small = dot(order, small)
    g3 = jnp.concatenate([small[48 * a : 48 * a + 48] for a in range(3)], axis=1).astype(BF16)
    flipped = [
        jnp.concatenate(
            [small[144 + 24 * a + 8 * d : 152 + 24 * a + 8 * d] for d in (2, 1, 0)], axis=0
        )
        for a in range(3)
    ]
    g1t = jnp.concatenate(flipped, axis=1).astype(BF16)
    eye = iota((16, 16), 0) == iota((16, 16), 1)
    b1, b2 = (
        jnp.sum(jnp.where(eye, jnp.broadcast_to(ref[...], (16, 16)), 0.0), axis=1, keepdims=True)
        for ref in (b1_ref, b2_ref)
    )
    bias1 = jnp.concatenate([b1] * 8, axis=0)
    bias2 = jnp.concatenate([b2] * 8, axis=0)

    for copy in first:
        copy.wait()
    if nx == 4:
        win[:, pl.ds(0, 256)] = win[:, pl.ds(1024, 256)]

    noise_all = win[...]
    parity = (iota((40, 1280), 0) >> 2) + iota((40, 1280), 0) + (iota((40, 1280), 1) >> 7) + iota((40, 1280), 1)
    inputs = jnp.where((parity & 1) == 0, noise_all, 0.0).astype(BF16).astype(F32)
    for d in range(3):
        inr[d] = roll_z(inputs, d - 1)
    for j in range(4):
        stack = jnp.concatenate(
            [
                inr[d, pl.ds(8 * j, 16), pl.ds(128 * a, 1024)]
                for d in range(3)
                for a in range(3)
            ],
            axis=0,
        ).astype(BF16)
        h1[pl.ds(128 * j, 128), :] = jnp.tanh(dot(g1[...], stack) + bias1).astype(BF16)

    def conv(mats, ref, start, width, rows):
        stack = [ref[pl.ds(start, 256), pl.ds(128 * a, width)] for a in range(3)]
        out = dot(mats[...], jnp.concatenate(stack, axis=0))
        total = out[rows : 2 * rows]
        for d in (0, 2):
            total = total + roll_z(out[d * rows : (d + 1) * rows], d - 1)
        return total

    for k in range(3):
        h2[pl.ds(128 * k, 128), :] = jnp.tanh(
            conv(g2, h1, 128 * k, 768, 128) + bias2
        ).astype(BF16)

    scales, growths = [], []
    for k in range(2):
        head = conv(g3, h2, 128 * k, 512, 16)
        log_scale = jnp.tanh(head[:8] + b3_ref[:, 0:1])
        offset = head[8:] + b3_ref[:, 1:2]
        noise = win[pl.ds(12 + 8 * k, 8), pl.ds(384, 512)]
        growth = jnp.exp(log_scale)
        r, l = iota((8, 512), 0), iota((8, 512), 1)
        even = (((r >> 2) + r + (l >> 7) + l) & 1) == 0
        fld[pl.ds(8 * k, 8), :] = jnp.where(even, noise, noise * growth + offset)
        scales.append(log_scale)
    log_scale = jnp.concatenate([scales[0][4:], scales[1][:4]], axis=0)[:, 128:384]
    growth = jnp.exp(log_scale)
    noise = win[pl.ds(16, 8), pl.ds(512, 256)]
    field = fld[pl.ds(4, 8), pl.ds(128, 256)]
    r, l = iota((8, 256), 0), iota((8, 256), 1)
    frozen = (((r >> 2) + r + (l >> 7) + l) & 1) == 0
    active = jnp.where(frozen, 0.0, 1.0)
    t_up = jnp.concatenate([field[1:4], field[0:1], field[5:8], field[4:5]], axis=0)
    t_down = jnp.concatenate([field[3:4], field[0:3], field[7:8], field[4:7]], axis=0)
    upward = (
        fld[pl.ds(4, 8), pl.ds(256, 256)] + fld[pl.ds(8, 8), pl.ds(128, 256)]
        + t_up + roll_z(field, 1)
    )
    downward = (
        fld[pl.ds(4, 8), pl.ds(0, 256)] + fld[pl.ds(0, 8), pl.ds(128, 256)]
        + t_down + roll_z(field, -1)
    )
    squared = field * field
    density = (
        -2.0 * HOPPING * field * upward + squared + QUARTIC * (squared - 1.0) * (squared - 1.0)
    )
    loss = jnp.sum(
        jnp.sum(-0.5 * noise * noise - active * log_scale + density, axis=1, keepdims=True),
        axis=0, keepdims=True,
    )
    force = (
        -2.0 * HOPPING * (upward + downward) + 2.0 * field + 4.0 * QUARTIC * field * (squared - 1.0)
    )
    d_scale = active * (force * noise * growth - 1.0) * (1.0 - log_scale * log_scale)
    d_offset = active * force
    cot_last = jnp.concatenate([d_scale, d_offset], axis=0).astype(BF16)
    clw[pl.ds(32, 16), pl.ds(512, 256)] = cot_last
    second = exchange(clw, 16, send_b, recv_b)
    for copy in second:
        copy.start()
    for x in range(2):
        for y in range(2):
            pack_ref[pl.ds(208 + 8 * x + 4 * y, 4), :] = field[4 * y : 4 * y + 4, 128 * x : 128 * x + 128]

    cot_f = cot_last.astype(F32)
    bias_last = jnp.sum(cot_f, axis=1, keepdims=True)
    bias_last = jnp.concatenate(
        [jnp.sum(bias_last[:8], axis=0, keepdims=True), jnp.sum(bias_last[8:], axis=0, keepdims=True)],
        axis=0,
    )
    turned = jnp.concatenate([roll_z(cot_f, 1 - d) for d in range(3)], axis=0).astype(BF16)
    row, col = iota((64, 48), 0), iota((64, 48), 1)
    order = jnp.where((row & 7) * 8 + (row >> 3) == col, 1.0, 0.0).astype(BF16)
    turned = dot(order, turned).astype(BF16)
    last_products = [
        dot_nt(turned, h2[pl.ds(64, 256), pl.ds(128 * (a + 1), 256)]) for a in range(3)
    ]

    for copy in second:
        copy.wait()
    if nx == 4:
        clw[:, pl.ds(0, 256)] = clw[:, pl.ds(1024, 256)]

    everywhere = clw[...].astype(F32)
    for d in range(3):
        clr[d] = roll_z(everywhere, d - 1).astype(BF16)
    for k in range(3):
        stack = jnp.concatenate(
            [
                clr[d, pl.ds(16 * k, 48), pl.ds(128 * (a + 1), 768)]
                for d in range(3)
                for a in range(3)
            ],
            axis=0,
        )
        hidden = h2[pl.ds(128 * k, 128), :].astype(F32)
        cm[pl.ds(128 * k, 128), :] = (dot(g3t[...], stack) * (1.0 - hidden * hidden)).astype(BF16)

    mine = cm[pl.ds(128, 128), pl.ds(256, 256)].astype(F32)
    bias_mid = jnp.sum(mine, axis=1, keepdims=True)
    bias_mid = sum(bias_mid[16 * n : 16 * n + 16] for n in range(8))
    turned = jnp.concatenate([roll_z(mine, 1 - d) for d in range(3)], axis=0).astype(BF16)
    products = [dot_nt(turned, h1[pl.ds(128, 256), pl.ds(128 * (a + 2), 256)]) for a in range(3)]
    pieces = []
    for n in range(8):
        pieces.append(
            jnp.concatenate(
                [
                    products[a][d * 128 + n * 16 : d * 128 + n * 16 + 16]
                    for a in range(3)
                    for d in range(3)
                ]
                + [last_products[a][8 * n : 8 * n + 8] for a in range(3)],
                axis=0,
            )
        )
    high, low = split(jnp.concatenate(pieces, axis=1))
    folded = dot_nt(high, tp[...]) + dot_nt(low, tp[...])
    partial_ref[pl.ds(0, 144), :] = folded[:144, :128].astype(BF16)
    partial_ref[pl.ds(144, 48), :] = jnp.concatenate(
        [
            folded[144:, :128],
            jnp.concatenate(
                [folded[24 * q : 24 * q + 24, 128:] for q in range(7)] + [jnp.zeros((24, 16), F32)],
                axis=1,
            ),
        ],
        axis=0,
    ).astype(BF16)
    for c in range(CHUNKS):
        contribute(c, partial_ref.at[pl.ds(16 * c, 16)], parts, recv_c)

    for k in range(2):
        hidden = h1[pl.ds(128 * (k + 1), 128), pl.ds(256, 512)].astype(F32)
        cf[pl.ds(128 * k, 128), :] = (
            conv(g2t, cm, 128 * k, 512, 128) * (1.0 - hidden * hidden)
        ).astype(BF16)
    mine = cf[pl.ds(64, 128), pl.ds(128, 256)]
    bias_first = jnp.sum(mine.astype(F32), axis=1, keepdims=True)
    bias_first = sum(bias_first[16 * n : 16 * n + 16] for n in range(8))
    stack = jnp.concatenate(
        [inr[d, pl.ds(12, 16), pl.ds(128 * (a + 3), 256)] for d in range(3) for a in range(3)], axis=0
    ).astype(BF16)
    product = dot_nt(mine, stack)
    folded = None
    for n, (y, t) in enumerate(PAIRS):
        high, low = split(product[16 * n : 16 * n + 16])
        matrix = taps_single(y, t)
        part = dot_nt(high, matrix) + dot_nt(low, matrix)
        folded = part if folded is None else folded + part
    pad = jnp.zeros((14, 1), F32)
    extra_ref[...] = jnp.concatenate(
        [
            folded, bias_mid, bias_first, jnp.concatenate([bias_last, pad], axis=0),
            jnp.concatenate([loss, pad, jnp.zeros((1, 1), F32)], axis=0), jnp.zeros((16, 43), F32),
        ],
        axis=1,
    )
    contribute(CHUNKS, extra_ref, extra_parts, recv_e)

    back = conv(g1t, cf, 0, 256, 8)
    result = jnp.where(frozen, back, 0.0) + force * jnp.where(frozen, 1.0, growth) - noise
    for x in range(2):
        for y in range(2):
            pack_ref[pl.ds(224 + 8 * x + 4 * y, 4), :] = result[4 * y : 4 * y + 4, 128 * x : 128 * x + 128]

    def add_up(own, buffer, result):
        summed = own.astype(F32)
        for k in range(devices - 1):
            summed = summed + buffer[pl.ds(16 * k, 16), :].astype(F32)
        return (summed / sites).astype(result)

    chunk = lax.div(me * (CHUNKS + 1) + devices - 1, devices)
    owns = (lax.div(chunk * devices, CHUNKS + 1) == me) & (chunk < CHUNKS)
    owns_extra = me == owner(CHUNKS)

    @pl.when(owns)
    def _():
        pltpu.make_async_copy(parts, parts, recv_c).wait()
        rows = pl.ds(pl.multiple_of(chunk * 16, 16), 16)
        total[rows, :] = add_up(partial_ref[rows, :], parts, BF16)
        share(chunk, total.at[rows], send_d)

    @pl.when(owns_extra)
    def _():
        pltpu.make_async_copy(extra_parts, extra_parts, recv_e).wait()
        extra_total[...] = add_up(extra_ref[...], extra_parts, F32)
        share(CHUNKS, extra_total, send_f)

    for c in range(CHUNKS + 1):
        @pl.when(me != owner(c))
        def _():
            sent = extra_ref if c == CHUNKS else partial_ref.at[pl.ds(16 * c, 16)]
            given = extra_total if c == CHUNKS else total.at[pl.ds(16 * c, 16)]
            pltpu.make_async_copy(sent, sent, send_c.at[c]).wait()
            pltpu.make_async_copy(given, given, recv_d.at[c]).wait()

    pack_ref[pl.ds(0, 192), :] = total[...].astype(F32)
    pack_ref[pl.ds(192, 16), :] = extra_total[...]

    @pl.when(owns)
    def _():
        pltpu.make_async_copy(parts, parts, send_d).wait()

    @pl.when(owns_extra)
    def _():
        pltpu.make_async_copy(extra_parts, extra_parts, send_f).wait()


def unpack(
    pack_ref,
    field_out, ngrad_out, loss_out, w1_out, b1_out, w2_out, b2_out, w3_out, b3_out,
):
    for x in range(2):
        for y in range(2):
            field_out[x, y] = pack_ref[pl.ds(208 + 8 * x + 4 * y, 4), :]
            ngrad_out[x, y] = pack_ref[pl.ds(224 + 8 * x + 4 * y, 4), :]
    last_taps = pack_ref[pl.ds(168, 24), :]
    last_taps = jnp.concatenate(
        [last_taps[:, 16 * q : 16 * q + 16] for q in range(7)], axis=0
    )

    def taps(start, rows, g):
        if g == 8:
            return last_taps[start : start + rows]
        return pack_ref[pl.ds(start, rows), :][:, 16 * g : 16 * g + 16]

    for a in range(3):
        for g in range(9):
            heads = taps(144 + 8 * a, 8, g)
            for d in range(3):
                w2_out[a, g // 3, g % 3, d] = taps((3 * a + d) * 16, 16, g)
                w3_out[a, g // 3, g % 3, d] = heads[2 * d : 2 * d + 2]
    extra = jnp.transpose(pack_ref[pl.ds(192, 16), :], (1, 0))
    for r in range(81):
        w1_out[r // 27, (r // 9) % 3, (r // 3) % 3, r % 3] = extra[r : r + 1]
    b2_out[...] = extra[81:82]
    b1_out[...] = extra[82:83]
    b3_out[...] = extra[83:84, :2]
    loss_out[...] = extra[84:85, :1]


def local(nx, ny, noise, w_first, b_first, w_middle, b_middle, w_last, b_last):
    sites = float(noise.size * nx * ny)
    vmem = pl.BlockSpec(memory_space=pltpu.VMEM)
    hbm = pl.BlockSpec(memory_space=pltpu.HBM)
    devices = nx * ny
    pack = pl.pallas_call(
        functools.partial(kernel, nx, ny, sites),
        out_shape=jax.ShapeDtypeStruct((240, 128), F32),
        in_specs=[hbm] * 7,
        out_specs=vmem,
        scratch_shapes=[
            pltpu.VMEM(noise.shape, F32),
            pltpu.VMEM((1, 3, 3, 3, 3, 16), BF16),
            pltpu.VMEM((1, 16), F32),
            pltpu.VMEM((3, 3, 3, 3, 16, 16), BF16),
            pltpu.VMEM((1, 16), F32),
            pltpu.VMEM((3, 3, 3, 3, 2, 16), BF16),
            pltpu.VMEM((1, 2), F32),
            pltpu.VMEM((320, 144), F32),
            pltpu.VMEM((128, 16), F32),
            pltpu.VMEM((256, 16), F32),
            pltpu.VMEM((40, 1280), F32),
            pltpu.VMEM((3, 40, 1280), F32),
            pltpu.VMEM((80, 1280), BF16),
            pltpu.VMEM((3, 80, 1280), BF16),
            pltpu.VMEM((384, 768), BF16),
            pltpu.VMEM((384, 768), BF16),
            pltpu.VMEM((128, 144), BF16),
            pltpu.VMEM((128, 432), BF16),
            pltpu.VMEM((512, 1024), BF16),
            pltpu.VMEM((384, 768), BF16),
            pltpu.VMEM((384, 768), BF16),
            pltpu.VMEM((256, 512), BF16),
            pltpu.VMEM((16, 512), F32),
            pltpu.VMEM((144, 2048), BF16),
            pltpu.VMEM((16 * CHUNKS, 128), BF16),
            pltpu.VMEM((16 * (devices - 1), 128), BF16),
            pltpu.VMEM((16 * CHUNKS, 128), BF16),
            pltpu.VMEM((16, 128), F32),
            pltpu.VMEM((16 * (devices - 1), 128), F32),
            pltpu.VMEM((16, 128), F32),
        ]
        + [pltpu.SemaphoreType.DMA((24,))] * 4
        + [pltpu.SemaphoreType.DMA((CHUNKS + 1,)), pltpu.SemaphoreType.DMA] * 2
        + [pltpu.SemaphoreType.DMA] * 2
        + [pltpu.SemaphoreType.DMA((7,))],
        compiler_params=pltpu.CompilerParams(
            collective_id=0, has_side_effects=True, vmem_limit_bytes=63 * 1024 * 1024
        ),
    )(
        noise, jnp.transpose(w_first, (1, 2, 3, 4, 5, 0)), b_first.reshape(1, 16),
        jnp.transpose(w_middle, (2, 3, 4, 5, 0, 1)), b_middle.reshape(1, 16),
        jnp.transpose(w_last, (2, 3, 4, 5, 0, 1)), b_last.reshape(1, 2),
    )
    field, ngrad, loss, first, bias1, middle, bias2, last, bias3 = pl.pallas_call(
        unpack,
        out_shape=(
            jax.ShapeDtypeStruct(noise.shape, F32),
            jax.ShapeDtypeStruct(noise.shape, F32),
            jax.ShapeDtypeStruct((1, 1), F32),
            jax.ShapeDtypeStruct((3, 3, 3, 3, 1, 16), F32),
            jax.ShapeDtypeStruct((1, 16), F32),
            jax.ShapeDtypeStruct((3, 3, 3, 3, 16, 16), F32),
            jax.ShapeDtypeStruct((1, 16), F32),
            jax.ShapeDtypeStruct((3, 3, 3, 3, 2, 16), F32),
            jax.ShapeDtypeStruct((1, 2), F32),
        ),
        in_specs=[vmem],
        out_specs=(vmem,) * 9,
    )(pack)
    order = (4, 5, 0, 1, 2, 3)
    return (
        field, ngrad, loss.reshape(()), jnp.transpose(first, (5, 4, 0, 1, 2, 3)),
        bias1.reshape(16), jnp.transpose(middle, order), bias2.reshape(16),
        jnp.transpose(last, order), bias3.reshape(2),
    )


def solution(mesh):
    placed = (P("gx", "gy", None, None), P(), P(), P(), P(), P(), P())
    return jax.shard_map(
        functools.partial(local, mesh.shape["gx"], mesh.shape["gy"]),
        mesh=mesh,
        in_specs=placed,
        out_specs=(
            P("gx", "gy", None, None), P("gx", "gy", None, None), P(), P(), P(), P(), P(), P(), P(),
        ),
        check_vma=False,
    )
```

```python
import functools

import jax
import jax.numpy as jnp
from jax import lax
from jax.experimental import pallas as pl
from jax.experimental.pallas import tpu as pltpu
from jax.sharding import PartitionSpec as P

HOPPING = 0.15
QUARTIC = 0.1
MESH = pl.DeviceIdType.MESH
F32 = jnp.float32
BF16 = jnp.bfloat16
OFFSETS = [(dx, dy) for dx in range(-2, 3) for dy in range(-2, 3) if (dx, dy) != (0, 0)]
CHUNKS = 12
PAIRS = [(y, t) for y in range(2) for t in range(4)]


def dot(a, b):
    return jnp.dot(a, b, preferred_element_type=F32)


def dot_nt(a, b):
    return lax.dot_general(a, b, (((1,), (1,)), ((), ())), preferred_element_type=F32)


def roll_z(v, step):
    if step == 0:
        return v
    parts = [
        pltpu.roll(v[:, k : k + 128], (-step) % 128, 1) for k in range(0, v.shape[1], 128)
    ]
    return parts[0] if len(parts) == 1 else jnp.concatenate(parts, axis=1)


def iota(shape, dim):
    return lax.broadcasted_iota(jnp.int32, shape, dim)


def select_matrix(rows, target):
    lanes = target.shape[1]
    return jnp.where(iota((rows, lanes), 0) == target, 1.0, 0.0).astype(BF16)


def taps_channels(y, t):
    lane = iota((1, 256), 1)
    b = (lane >> 6) - y
    c = (((lane >> 4) & 3) - t + 1) & 3
    ok = (b >= 0) & (b <= 2) & (c <= 2)
    return select_matrix(144, jnp.where(ok, b * 48 + c * 16 + (lane & 15), -1))


def taps_single(y, t):
    lane = iota((1, 144), 1)
    d = (lane >= 48).astype(jnp.int32) + (lane >= 96).astype(jnp.int32)
    b = ((lane >> 2) & 3) - y
    c = ((lane & 3) - t + 1) & 3
    ok = (b >= 0) & (b <= 2) & (c <= 2)
    return select_matrix(81, jnp.where(ok, ((lane >> 4) - 3 * d) * 27 + b * 9 + c * 3 + d, -1))


def taps_heads(y, t):
    lane = iota((1, 432), 1)
    group = sum((lane >= 48 * k).astype(jnp.int32) for k in range(1, 9))
    rest = lane - 48 * group
    b = 2 * (rest >> 4) + ((rest >> 2) & 1) - y - 1
    c = ((rest & 3) - t + 1) & 3
    ok = (b >= 0) & (b <= 2) & (c <= 2)
    target = group * 18 + b * 6 + c * 2 + ((rest >> 3) & 1)
    return select_matrix(162, jnp.where(ok, target, -1))


def split(v):
    high = v.astype(BF16)
    return high, (v - high.astype(F32)).astype(BF16)


def kernel(
    nx, ny, sites, noise_hbm, w1_hbm, b1_hbm, w2_hbm, b2_hbm, w3_hbm, b3_hbm,
    pack_ref,
    noise_ref, w1_ref, b1_ref, w2_ref, b2_ref, w3_ref, b3_ref, wall_ref, w1_rows, w3_rows,
    win, inr, clw, clr, g2, g2t, g1, g3t, h1, h2, cm, cf, fld, tp, ts,
    partial_ref, parts, total, extra_ref, extra_parts, extra_total,
    send_a, recv_a, send_b, recv_b, send_c, recv_c, recv_d, send_d, recv_e, send_f, load,
):
    ix, iy = lax.axis_index("gx"), lax.axis_index("gy")
    devices = nx * ny
    me = ix * ny + iy

    def place(index):
        return (lax.div(index, ny), lax.rem(index, ny))

    def owner(c):
        return c * devices // (CHUNKS + 1)

    def contribute(c, source, buffer, arrived):
        @pl.when(me != owner(c))
        def _():
            slot = lax.rem(me - owner(c) - 1 + devices, devices)
            pltpu.make_async_remote_copy(
                src_ref=source,
                dst_ref=buffer.at[pl.ds(pl.multiple_of(slot * 16, 16), 16)],
                send_sem=send_c.at[c],
                recv_sem=arrived,
                device_id=(owner(c) // ny, owner(c) % ny),
                device_id_type=MESH,
            ).start()

    def share(c, ref, sent):
        def step(k, _):
            pltpu.make_async_remote_copy(
                src_ref=ref,
                dst_ref=ref,
                send_sem=sent,
                recv_sem=recv_d.at[c],
                device_id=place(lax.rem(me + k, devices)),
                device_id_type=MESH,
            ).start()
            return 0

        lax.fori_loop(1, devices, step, 0)

    def peer(dx, dy):
        return (lax.rem(ix + dx + 2 * nx, nx), lax.rem(iy + dy + 2 * ny, ny))

    def exchange(ref, rows, send, recv):
        copies = []
        for k, (dx, dy) in enumerate(OFFSETS):
            if dx == 2 and nx == 4:
                continue
            copies.append(
                pltpu.make_async_remote_copy(
                    src_ref=ref.at[pl.ds(2 * rows, rows), pl.ds(512, 256)],
                    dst_ref=ref.at[pl.ds((2 - dy) * rows, rows), pl.ds((2 - dx) * 256, 256)],
                    send_sem=send.at[k],
                    recv_sem=recv.at[k],
                    device_id=peer(dx, dy),
                    device_id_type=MESH,
                )
            )
        return copies

    loads = [
        pltpu.make_async_copy(source, target, load.at[k])
        for k, (source, target) in enumerate(
            [
                (noise_hbm, noise_ref), (w1_hbm, w1_ref), (b1_hbm, b1_ref), (w2_hbm, w2_ref),
                (b2_hbm, b2_ref), (w3_hbm, w3_ref), (b3_hbm, b3_ref),
            ]
        )
    ]
    for copy in loads:
        copy.start()
    barrier = pltpu.get_barrier_semaphore()

    def greet(k, _):
        pl.semaphore_signal(
            barrier, inc=1, device_id=place(lax.rem(me + k, devices)), device_id_type=MESH
        )
        return 0

    lax.fori_loop(1, devices, greet, 0)
    loads[0].wait()
    for x in range(2):
        for y in range(2):
            win[pl.ds(16 + 4 * y, 4), pl.ds(512 + 128 * x, 128)] = noise_ref[x, y]
    pl.semaphore_wait(barrier, devices - 1)
    first = exchange(win, 8, send_a, recv_a)
    for copy in first:
        copy.start()

    for copy in loads[1:]:
        copy.wait()
    wall_ref[pl.ds(304, 16), :] = jnp.zeros((16, 144), F32)
    for a in range(3):
        for d in range(3):
            slabs = [w2_ref[a, g // 3, g % 3, d].astype(F32) for g in range(9)]
            wall_ref[pl.ds(16 * (3 * a + d), 16), :] = jnp.concatenate(slabs, axis=1)
            heads = [w3_ref[a, g // 3, g % 3, d].astype(F32) for g in range(9)]
            wall_ref[pl.ds(288 + 2 * (3 * a + d), 2), :] = jnp.concatenate(heads, axis=1)
            for g in range(9):
                w3_rows[pl.ds((3 * (2 - d) + 2 - a) * 18 + 2 * (8 - g), 2), :] = heads[g]
        for g in range(9):
            row = w1_ref[0, a, g // 3, g % 3].astype(F32)
            w1_rows[pl.ds(27 * a + 3 * g, 3), :] = row
            wall_ref[pl.ds(306 + 3 * (2 - a), 3), pl.ds(16 * (8 - g), 16)] = row
    wall = jnp.concatenate(
        [wall_ref[pl.ds(0, 144), :], wall_ref[pl.ds(288, 32), :]], axis=0
    ).astype(BF16)
    w1 = jnp.transpose(w1_rows[...], (1, 0))[:, :81].astype(BF16)
    small = []
    for n, (y, t) in enumerate(PAIRS):
        matrix = taps_channels(y, t)
        tp[:, pl.ds(256 * n, 256)] = matrix
        full = dot(wall, matrix).astype(BF16)
        for a in range(3):
            for d in range(3):
                where = (pl.ds(d * 128 + n * 16, 16), pl.ds(256 * a, 256))
                g2[where] = full[(3 * a + d) * 16 : (3 * a + d) * 16 + 16]
        small.append(full[144:176])
        single = taps_single(y, t)
        ts[n] = single
        g1[pl.ds(n * 16, 16), :] = dot(w1, single).astype(BF16)
    small = jnp.concatenate(small, axis=0)
    row = iota((216, 256), 0)
    order = jnp.where((row & 7) * 32 + (row >> 3) == iota((216, 256), 1), 1.0, 0.0).astype(BF16)
    small = dot(order, small)
    g3 = jnp.concatenate([small[48 * a : 48 * a + 48] for a in range(3)], axis=1).astype(BF16)
    flipped = [
        jnp.concatenate(
            [small[144 + 24 * a + 8 * d : 152 + 24 * a + 8 * d] for d in (2, 1, 0)], axis=0
        )
        for a in range(3)
    ]
    g1t = jnp.concatenate(flipped, axis=1).astype(BF16)
    eye = iota((16, 16), 0) == iota((16, 16), 1)
    b1, b2 = (
        jnp.sum(jnp.where(eye, jnp.broadcast_to(ref[...], (16, 16)), 0.0), axis=1, keepdims=True)
        for ref in (b1_ref, b2_ref)
    )
    bias1 = jnp.concatenate([b1] * 8, axis=0)
    bias2 = jnp.concatenate([b2] * 8, axis=0)

    for copy in first:
        copy.wait()
    if nx == 4:
        win[:, pl.ds(0, 256)] = win[:, pl.ds(1024, 256)]

    noise_all = win[...]
    parity = (iota((40, 1280), 0) >> 2) + iota((40, 1280), 0) + (iota((40, 1280), 1) >> 7) + iota((40, 1280), 1)
    inputs = jnp.where((parity & 1) == 0, noise_all, 0.0).astype(BF16).astype(F32)
    for d in range(3):
        inr[d] = roll_z(inputs, d - 1)
    for j in range(4):
        stack = jnp.concatenate(
            [
                inr[d, pl.ds(8 * j, 16), pl.ds(128 * a, 1024)]
                for d in range(3)
                for a in range(3)
            ],
            axis=0,
        ).astype(BF16)
        h1[pl.ds(128 * j, 128), :] = jnp.tanh(dot(g1[...], stack) + bias1).astype(BF16)

    def conv(mats, ref, start, width, rows):
        stack = [ref[pl.ds(start, 256), pl.ds(128 * a, width)] for a in range(3)]
        out = dot(mats[...], jnp.concatenate(stack, axis=0))
        total = out[rows : 2 * rows]
        for d in (0, 2):
            total = total + roll_z(out[d * rows : (d + 1) * rows], d - 1)
        return total

    for k in range(3):
        h2[pl.ds(128 * k, 128), :] = jnp.tanh(
            conv(g2, h1, 128 * k, 768, 128) + bias2
        ).astype(BF16)

    scales, growths = [], []
    for k in range(2):
        head = conv(g3, h2, 128 * k, 512, 16)
        log_scale = jnp.tanh(head[:8] + b3_ref[:, 0:1])
        offset = head[8:] + b3_ref[:, 1:2]
        noise = win[pl.ds(12 + 8 * k, 8), pl.ds(384, 512)]
        growth = jnp.exp(log_scale)
        r, l = iota((8, 512), 0), iota((8, 512), 1)
        even = (((r >> 2) + r + (l >> 7) + l) & 1) == 0
        fld[pl.ds(8 * k, 8), :] = jnp.where(even, noise, noise * growth + offset)
        scales.append(log_scale)
    log_scale = jnp.concatenate([scales[0][4:], scales[1][:4]], axis=0)[:, 128:384]
    growth = jnp.exp(log_scale)
    noise = win[pl.ds(16, 8), pl.ds(512, 256)]
    field = fld[pl.ds(4, 8), pl.ds(128, 256)]
    r, l = iota((8, 256), 0), iota((8, 256), 1)
    frozen = (((r >> 2) + r + (l >> 7) + l) & 1) == 0
    active = jnp.where(frozen, 0.0, 1.0)
    t_up = jnp.concatenate([field[1:4], field[0:1], field[5:8], field[4:5]], axis=0)
    t_down = jnp.concatenate([field[3:4], field[0:3], field[7:8], field[4:7]], axis=0)
    upward = (
        fld[pl.ds(4, 8), pl.ds(256, 256)] + fld[pl.ds(8, 8), pl.ds(128, 256)]
        + t_up + roll_z(field, 1)
    )
    downward = (
        fld[pl.ds(4, 8), pl.ds(0, 256)] + fld[pl.ds(0, 8), pl.ds(128, 256)]
        + t_down + roll_z(field, -1)
    )
    squared = field * field
    density = (
        -2.0 * HOPPING * field * upward + squared + QUARTIC * (squared - 1.0) * (squared - 1.0)
    )
    loss = jnp.sum(
        jnp.sum(-0.5 * noise * noise - active * log_scale + density, axis=1, keepdims=True),
        axis=0, keepdims=True,
    )
    force = (
        -2.0 * HOPPING * (upward + downward) + 2.0 * field + 4.0 * QUARTIC * field * (squared - 1.0)
    )
    d_scale = active * (force * noise * growth - 1.0) * (1.0 - log_scale * log_scale)
    d_offset = active * force
    cot_last = jnp.concatenate([d_scale, d_offset], axis=0).astype(BF16)
    clw[pl.ds(32, 16), pl.ds(512, 256)] = cot_last
    second = exchange(clw, 16, send_b, recv_b)
    for copy in second:
        copy.start()
    for x in range(2):
        for y in range(2):
            pack_ref[pl.ds(208 + 8 * x + 4 * y, 4), :] = field[4 * y : 4 * y + 4, 128 * x : 128 * x + 128]

    cot_f = cot_last.astype(F32)
    bias_last = jnp.sum(cot_f, axis=1, keepdims=True)
    bias_last = jnp.concatenate(
        [jnp.sum(bias_last[:8], axis=0, keepdims=True), jnp.sum(bias_last[8:], axis=0, keepdims=True)],
        axis=0,
    )
    turned = jnp.concatenate([roll_z(cot_f, 1 - d) for d in range(3)], axis=0).astype(BF16)
    row, col = iota((64, 48), 0), iota((64, 48), 1)
    order = jnp.where((row & 7) * 8 + (row >> 3) == col, 1.0, 0.0).astype(BF16)
    turned = dot(order, turned).astype(BF16)
    last_products = [
        dot_nt(turned, h2[pl.ds(64, 256), pl.ds(128 * (a + 1), 256)]) for a in range(3)
    ]

    for a in range(3):
        for d in range(3):
            slabs = [w2_ref[a, g // 3, g % 3, d].astype(F32) for g in range(8, -1, -1)]
            wall_ref[pl.ds(144 + 16 * (3 * (2 - a) + 2 - d), 16), :] = jnp.transpose(
                jnp.concatenate(slabs, axis=0), (1, 0)
            )
    wall = wall_ref[pl.ds(144, 144), :].astype(BF16)
    w3t = jnp.transpose(w3_rows[...], (1, 0))[:, :162].astype(BF16)
    for n, (y, t) in enumerate(PAIRS):
        full = dot(wall, tp[:, pl.ds(256 * n, 256)]).astype(BF16)
        for a in range(3):
            for d in range(3):
                where = (pl.ds(d * 128 + n * 16, 16), pl.ds(256 * a, 256))
                g2t[where] = full[(3 * a + d) * 16 : (3 * a + d) * 16 + 16]
        g3t[pl.ds(n * 16, 16), :] = dot(w3t, taps_heads(y, t)).astype(BF16)

    for copy in second:
        copy.wait()
    if nx == 4:
        clw[:, pl.ds(0, 256)] = clw[:, pl.ds(1024, 256)]

    everywhere = clw[...].astype(F32)
    for d in range(3):
        clr[d] = roll_z(everywhere, d - 1).astype(BF16)
    for k in range(3):
        stack = jnp.concatenate(
            [
                clr[d, pl.ds(16 * k, 48), pl.ds(128 * (a + 1), 768)]
                for d in range(3)
                for a in range(3)
            ],
            axis=0,
        )
        hidden = h2[pl.ds(128 * k, 128), :].astype(F32)
        cm[pl.ds(128 * k, 128), :] = (dot(g3t[...], stack) * (1.0 - hidden * hidden)).astype(BF16)

    mine = cm[pl.ds(128, 128), pl.ds(256, 256)].astype(F32)
    bias_mid = jnp.sum(mine, axis=1, keepdims=True)
    bias_mid = sum(bias_mid[16 * n : 16 * n + 16] for n in range(8))
    turned = jnp.concatenate([roll_z(mine, 1 - d) for d in range(3)], axis=0).astype(BF16)
    products = [dot_nt(turned, h1[pl.ds(128, 256), pl.ds(128 * (a + 2), 256)]) for a in range(3)]
    pieces = []
    for n in range(8):
        pieces.append(
            jnp.concatenate(
                [
                    products[a][d * 128 + n * 16 : d * 128 + n * 16 + 16]
                    for a in range(3)
                    for d in range(3)
                ]
                + [last_products[a][8 * n : 8 * n + 8] for a in range(3)],
                axis=0,
            )
        )
    high, low = split(jnp.concatenate(pieces, axis=1))
    folded = dot_nt(high, tp[...]) + dot_nt(low, tp[...])
    partial_ref[pl.ds(0, 144), :] = folded[:144, :128].astype(BF16)
    partial_ref[pl.ds(144, 48), :] = jnp.concatenate(
        [
            folded[144:, :128],
            jnp.concatenate(
                [folded[24 * q : 24 * q + 24, 128:] for q in range(7)] + [jnp.zeros((24, 16), F32)],
                axis=1,
            ),
        ],
        axis=0,
    ).astype(BF16)
    for c in range(CHUNKS):
        contribute(c, partial_ref.at[pl.ds(16 * c, 16)], parts, recv_c)

    for k in range(2):
        hidden = h1[pl.ds(128 * (k + 1), 128), pl.ds(256, 512)].astype(F32)
        cf[pl.ds(128 * k, 128), :] = (
            conv(g2t, cm, 128 * k, 512, 128) * (1.0 - hidden * hidden)
        ).astype(BF16)
    mine = cf[pl.ds(64, 128), pl.ds(128, 256)]
    bias_first = jnp.sum(mine.astype(F32), axis=1, keepdims=True)
    bias_first = sum(bias_first[16 * n : 16 * n + 16] for n in range(8))
    stack = jnp.concatenate(
        [inr[d, pl.ds(12, 16), pl.ds(128 * (a + 3), 256)] for d in range(3) for a in range(3)], axis=0
    ).astype(BF16)
    product = dot_nt(mine, stack)
    folded = None
    for n, (y, t) in enumerate(PAIRS):
        high, low = split(product[16 * n : 16 * n + 16])
        matrix = ts[n]
        part = dot_nt(high, matrix) + dot_nt(low, matrix)
        folded = part if folded is None else folded + part
    pad = jnp.zeros((14, 1), F32)
    extra_ref[...] = jnp.concatenate(
        [
            folded, bias_mid, bias_first, jnp.concatenate([bias_last, pad], axis=0),
            jnp.concatenate([loss, pad, jnp.zeros((1, 1), F32)], axis=0), jnp.zeros((16, 43), F32),
        ],
        axis=1,
    )
    contribute(CHUNKS, extra_ref, extra_parts, recv_e)

    def add_up(own, buffer, result):
        summed = own.astype(F32)
        for k in range(devices - 1):
            summed = summed + buffer[pl.ds(16 * k, 16), :].astype(F32)
        return (summed / sites).astype(result)

    chunk = lax.div(me * (CHUNKS + 1) + devices - 1, devices)
    owns = (lax.div(chunk * devices, CHUNKS + 1) == me) & (chunk < CHUNKS)
    owns_extra = me == owner(CHUNKS)

    @pl.when(owns)
    def _():
        pltpu.make_async_copy(parts, parts, recv_c).wait()
        rows = pl.ds(pl.multiple_of(chunk * 16, 16), 16)
        total[rows, :] = add_up(partial_ref[rows, :], parts, BF16)
        share(chunk, total.at[rows], send_d)

    back = conv(g1t, cf, 0, 256, 8)
    result = jnp.where(frozen, back, 0.0) + force * jnp.where(frozen, 1.0, growth) - noise
    for x in range(2):
        for y in range(2):
            pack_ref[pl.ds(224 + 8 * x + 4 * y, 4), :] = result[4 * y : 4 * y + 4, 128 * x : 128 * x + 128]

    @pl.when(owns_extra)
    def _():
        pltpu.make_async_copy(extra_parts, extra_parts, recv_e).wait()
        extra_total[...] = add_up(extra_ref[...], extra_parts, F32)
        share(CHUNKS, extra_total, send_f)

    for c in range(CHUNKS + 1):
        @pl.when(me != owner(c))
        def _():
            sent = extra_ref if c == CHUNKS else partial_ref.at[pl.ds(16 * c, 16)]
            given = extra_total if c == CHUNKS else total.at[pl.ds(16 * c, 16)]
            pltpu.make_async_copy(sent, sent, send_c.at[c]).wait()
            pltpu.make_async_copy(given, given, recv_d.at[c]).wait()

    pack_ref[pl.ds(0, 192), :] = total[...].astype(F32)
    pack_ref[pl.ds(192, 16), :] = extra_total[...]

    @pl.when(owns)
    def _():
        pltpu.make_async_copy(parts, parts, send_d).wait()

    @pl.when(owns_extra)
    def _():
        pltpu.make_async_copy(extra_parts, extra_parts, send_f).wait()


def unpack(
    pack_ref,
    field_out, ngrad_out, loss_out, w1_out, b1_out, w2_out, b2_out, w3_out, b3_out,
):
    for x in range(2):
        for y in range(2):
            field_out[x, y] = pack_ref[pl.ds(208 + 8 * x + 4 * y, 4), :]
            ngrad_out[x, y] = pack_ref[pl.ds(224 + 8 * x + 4 * y, 4), :]
    last_taps = pack_ref[pl.ds(168, 24), :]
    last_taps = jnp.concatenate(
        [last_taps[:, 16 * q : 16 * q + 16] for q in range(7)], axis=0
    )

    def taps(start, rows, g):
        if g == 8:
            return last_taps[start : start + rows]
        return pack_ref[pl.ds(start, rows), :][:, 16 * g : 16 * g + 16]

    for a in range(3):
        for g in range(9):
            heads = taps(144 + 8 * a, 8, g)
            for d in range(3):
                w2_out[a, g // 3, g % 3, d] = taps((3 * a + d) * 16, 16, g)
                w3_out[a, g // 3, g % 3, d] = heads[2 * d : 2 * d + 2]
    extra = jnp.transpose(pack_ref[pl.ds(192, 16), :], (1, 0))
    for r in range(81):
        w1_out[r // 27, (r // 9) % 3, (r // 3) % 3, r % 3] = extra[r : r + 1]
    b2_out[...] = extra[81:82]
    b1_out[...] = extra[82:83]
    b3_out[...] = extra[83:84, :2]
    loss_out[...] = extra[84:85, :1]


def local(nx, ny, noise, w_first, b_first, w_middle, b_middle, w_last, b_last):
    sites = float(noise.size * nx * ny)
    vmem = pl.BlockSpec(memory_space=pltpu.VMEM)
    hbm = pl.BlockSpec(memory_space=pltpu.HBM)
    devices = nx * ny
    pack = pl.pallas_call(
        functools.partial(kernel, nx, ny, sites),
        out_shape=jax.ShapeDtypeStruct((240, 128), F32),
        in_specs=[hbm] * 7,
        out_specs=vmem,
        scratch_shapes=[
            pltpu.VMEM(noise.shape, F32),
            pltpu.VMEM((1, 3, 3, 3, 3, 16), BF16),
            pltpu.VMEM((1, 16), F32),
            pltpu.VMEM((3, 3, 3, 3, 16, 16), BF16),
            pltpu.VMEM((1, 16), F32),
            pltpu.VMEM((3, 3, 3, 3, 2, 16), BF16),
            pltpu.VMEM((1, 2), F32),
            pltpu.VMEM((320, 144), F32),
            pltpu.VMEM((128, 16), F32),
            pltpu.VMEM((256, 16), F32),
            pltpu.VMEM((40, 1280), F32),
            pltpu.VMEM((3, 40, 1280), F32),
            pltpu.VMEM((80, 1280), BF16),
            pltpu.VMEM((3, 80, 1280), BF16),
            pltpu.VMEM((384, 768), BF16),
            pltpu.VMEM((384, 768), BF16),
            pltpu.VMEM((128, 144), BF16),
            pltpu.VMEM((128, 432), BF16),
            pltpu.VMEM((512, 1024), BF16),
            pltpu.VMEM((384, 768), BF16),
            pltpu.VMEM((384, 768), BF16),
            pltpu.VMEM((256, 512), BF16),
            pltpu.VMEM((16, 512), F32),
            pltpu.VMEM((144, 2048), BF16),
            pltpu.VMEM((8, 81, 144), BF16),
            pltpu.VMEM((16 * CHUNKS, 128), BF16),
            pltpu.VMEM((16 * (devices - 1), 128), BF16),
            pltpu.VMEM((16 * CHUNKS, 128), BF16),
            pltpu.VMEM((16, 128), F32),
            pltpu.VMEM((16 * (devices - 1), 128), F32),
            pltpu.VMEM((16, 128), F32),
        ]
        + [pltpu.SemaphoreType.DMA((24,))] * 4
        + [pltpu.SemaphoreType.DMA((CHUNKS + 1,)), pltpu.SemaphoreType.DMA] * 2
        + [pltpu.SemaphoreType.DMA] * 2
        + [pltpu.SemaphoreType.DMA((7,))],
        compiler_params=pltpu.CompilerParams(
            collective_id=0, has_side_effects=True, vmem_limit_bytes=63 * 1024 * 1024
        ),
    )(
        noise, jnp.transpose(w_first, (1, 2, 3, 4, 5, 0)), b_first.reshape(1, 16),
        jnp.transpose(w_middle, (2, 3, 4, 5, 0, 1)), b_middle.reshape(1, 16),
        jnp.transpose(w_last, (2, 3, 4, 5, 0, 1)), b_last.reshape(1, 2),
    )
    field, ngrad, loss, first, bias1, middle, bias2, last, bias3 = pl.pallas_call(
        unpack,
        out_shape=(
            jax.ShapeDtypeStruct(noise.shape, F32),
            jax.ShapeDtypeStruct(noise.shape, F32),
            jax.ShapeDtypeStruct((1, 1), F32),
            jax.ShapeDtypeStruct((3, 3, 3, 3, 1, 16), F32),
            jax.ShapeDtypeStruct((1, 16), F32),
            jax.ShapeDtypeStruct((3, 3, 3, 3, 16, 16), F32),
            jax.ShapeDtypeStruct((1, 16), F32),
            jax.ShapeDtypeStruct((3, 3, 3, 3, 2, 16), F32),
            jax.ShapeDtypeStruct((1, 2), F32),
        ),
        in_specs=[vmem],
        out_specs=(vmem,) * 9,
    )(pack)
    order = (4, 5, 0, 1, 2, 3)
    return (
        field, ngrad, loss.reshape(()), jnp.transpose(first, (5, 4, 0, 1, 2, 3)),
        bias1.reshape(16), jnp.transpose(middle, order), bias2.reshape(16),
        jnp.transpose(last, order), bias3.reshape(2),
    )


def solution(mesh):
    placed = (P("gx", "gy", None, None), P(), P(), P(), P(), P(), P())
    return jax.shard_map(
        functools.partial(local, mesh.shape["gx"], mesh.shape["gy"]),
        mesh=mesh,
        in_specs=placed,
        out_specs=(
            P("gx", "gy", None, None), P("gx", "gy", None, None), P(), P(), P(), P(), P(), P(), P(),
        ),
        check_vma=False,
    )
```
